128 devices in a mesh: step: 8 (over y, x_lo), head: 8 (over z, core), fsdp: 2 (over x_hi).
Axes of the slice: x: 4 (x_hi: 2, x_lo: 2; x = x_hi * 2 + x_lo), y: 4, z: 4, core: 2. Of those that a mesh axis runs over, the one named last changes fastest.
Arguments:
- states: float32 [8, 2, 1024, 5120], P('step', 'fsdp', 'head'), may hold values from -10.5 to 10.5
- timesteps: int32 [8, 2], P('step'), may hold values from 0 to 1000, as said below
- lengths: int32 [2], P('fsdp'), may hold values from 512 to 1024, as said below
- modulation: float32 [8, 3, 5120], P('step'), may hold values from -4 to 4
- w_query: bfloat16 [5120, 3072], P(('step', 'fsdp'), 'head'), may hold values from -0.1118034 to 0.1118034
- w_key: bfloat16 [5120, 3072], P(('step', 'fsdp'), 'head'), may hold values from -0.1118034 to 0.1118034
- w_value: bfloat16 [5120, 3072], P(('step', 'fsdp'), 'head'), may hold values from -0.078125 to 0.078125
- w_out: bfloat16 [3072, 5120], P('head', ('step', 'fsdp')), may hold values from -0.109375 to 0.109375
- q_gain: float32 [3072], P('head'), may hold values from 0.5 to 12
- k_gain: float32 [3072], P('head'), may hold values from 0.5 to 12
Outputs:
- next_states: float32 [8, 2, 1024, 5120], P('step', 'fsdp', 'head')
- update: bfloat16 [8, 2, 1024, 5120], P('step', 'fsdp', 'head')
The draws below stay inside these ranges and needn't reach their ends.
Inputs may be any that keep to these rules, and one draw needn't show every extreme that they name: `timesteps`: A row holds a step's start above its end; each row's end is the next row's start; the first row starts at 1000 and the last ends at 0. `lengths`: positions from a clip's length on are padding; at least one clip is full.
All inputs are finite; a program needn't handle non-finite values.
Results may differ from the reference program's by a relative error of at most 0.02.
The reference program's roundings to bfloat16 on the way count: a program that leaves them out, or rounds other values in their place, can miss the bound.
Values may be sent and summed in bfloat16 or wider, within the bound.
A program may use at most 128 MiB of HBM per device.

```python
import math
import jax
import jax.numpy as jnp
from jax import lax

D = 5120
HD = 128
HEADS = 24
INNER = 3072
SEQ = 1024
STEPS = 8
PROMPTS = 2
N_HEAD = 8


def draw_states(key, part):
    key = jax.random.fold_in(key, 11)
    base_key, row_key, col_key = jax.random.split(key, 3)
    shape_all = (STEPS, PROMPTS, SEQ, D)
    noise = jax.random.truncated_normal(base_key, -3.0, 3.0, shape_all, jnp.float32)
    row_scale = jnp.exp(jax.random.uniform(row_key, (STEPS, PROMPTS, SEQ, 1), jnp.float32, math.log(0.3), math.log(3.0)))
    col_scale = jnp.exp(jax.random.uniform(col_key, (1, 1, 1, D), jnp.float32, math.log(0.4), math.log(4.0)))
    return 0.2 * noise * row_scale * col_scale


def draw_timesteps(key, part):
    key = jax.random.fold_in(key, 23)
    widths = jax.random.randint(key, (STEPS,), 2, 5, dtype=jnp.int32)
    reached = jnp.cumsum(widths, dtype=jnp.int32)
    ends = (1000 - 1000 * reached // reached[-1]).astype(jnp.int32)
    starts = jnp.concatenate([jnp.full((1,), 1000, jnp.int32), ends[:-1]])
    return jnp.stack([starts, ends], axis=1).astype(jnp.int32)


def draw_lengths(key, part):
    key = jax.random.fold_in(key, 37)
    base_key, full_key = jax.random.split(key, 2)
    drawn = jax.random.randint(base_key, (PROMPTS,), SEQ // 2, SEQ + 1, dtype=jnp.int32)
    chosen = jax.random.randint(full_key, (), 0, PROMPTS, dtype=jnp.int32)
    return jnp.where(jnp.arange(PROMPTS, dtype=jnp.int32) == chosen, SEQ, drawn).astype(jnp.int32)


def draw_modulation(key, part):
    key = jax.random.fold_in(key, 67)
    base_key, sign_key, size_key = jax.random.split(key, 3)
    leading = 0.6 * jax.random.truncated_normal(base_key, -6.0, 6.0, (STEPS, 2, D), jnp.float32)
    magnitude = jnp.exp(jax.random.uniform(size_key, (STEPS, 1, D), jnp.float32, math.log(2.5), math.log(4.0)))
    signs = jnp.where(jax.random.bernoulli(sign_key, 0.5, (STEPS, 1, D)), 1.0, -1.0).astype(jnp.float32)
    return jnp.concatenate([leading, signs * magnitude], axis=1)


def rising_matrix(key, rise):
    entries = jax.random.truncated_normal(key, -4.0, 4.0, (D, INNER), jnp.float32)
    place = jnp.arange(INNER, dtype=jnp.float32) / float(INNER - 1) - 0.5
    column_scale = jnp.exp(math.log(rise) * place)
    return entries * column_scale[None, :] / math.sqrt(D)


def draw_w_query(key, part):
    key = jax.random.fold_in(key, 53)
    result = rising_matrix(key, 2.5)
    return result.astype(jnp.bfloat16)


def draw_w_key(key, part):
    key = jax.random.fold_in(key, 59)
    result = rising_matrix(key, 2.5)
    return result.astype(jnp.bfloat16)


def draw_q_gain(key, part):
    key = jax.random.fold_in(key, 41)
    result = jnp.exp(jax.random.uniform(key, (INNER,), jnp.float32, math.log(2.0), math.log(4.0)))
    return result


def draw_k_gain(key, part):
    key = jax.random.fold_in(key, 43)
    result = jnp.exp(jax.random.uniform(key, (INNER,), jnp.float32, math.log(2.0), math.log(4.0)))
    return result


def level_of(own_key, shape, pieces, least, largest):
    gain = 1.0
    for position, shards_of in pieces:
        steps = jax.random.uniform(jax.random.fold_in(jax.random.fold_in(own_key, 6), position), (shards_of,), jnp.float32, least / len(pieces), largest / len(pieces))
        gain = gain * jnp.repeat(jnp.exp(steps), shape[position] // shards_of).reshape((-1,) + (1,) * (len(shape) - 1 - position))
    return gain


def normal_values(stream_key, shape, deviation, bound, shards=(), held_as=jnp.bfloat16):
    values = deviation * jax.random.normal(stream_key, shape, jnp.float32)
    if shards:
        values = values * level_of(stream_key, shape, shards, -0.22, 0.18)
    return jnp.clip(values, -bound, bound).astype(held_as)


def setup_inputs(seed: int = 0) -> dict:
    streams_of = jax.random.split(jax.random.key(seed), 11)
    states = draw_states(jax.random.fold_in(streams_of[10], 71), 0)
    timesteps = draw_timesteps(jax.random.fold_in(streams_of[10], 71), 0)
    lengths = draw_lengths(jax.random.fold_in(streams_of[10], 71), 0)
    modulation = draw_modulation(jax.random.fold_in(streams_of[10], 71), 0)
    w_query = draw_w_query(jax.random.fold_in(streams_of[10], 71), 0)
    w_key = draw_w_key(jax.random.fold_in(streams_of[10], 71), 0)
    w_value = normal_values(streams_of[6], (D, INNER), D ** -0.5, 0.078125, ((0, 16), (1, 8)))
    w_out = normal_values(streams_of[7], (INNER, D), INNER ** -0.5, 0.109375, ((0, 8), (1, 16)))
    q_gain = draw_q_gain(jax.random.fold_in(streams_of[10], 71), 0)
    k_gain = draw_k_gain(jax.random.fold_in(streams_of[10], 71), 0)
    return dict(states=states, timesteps=timesteps, lengths=lengths, modulation=modulation, w_query=w_query, w_key=w_key, w_value=w_value, w_out=w_out, q_gain=q_gain, k_gain=k_gain)


def normed_rows(current, shift_row, scale_row):
    centre = lax.optimization_barrier(jnp.mean(current, axis=-1, keepdims=True))
    centred = current - centre
    spread = lax.optimization_barrier(jnp.mean(centred * centred, axis=-1, keepdims=True))
    return (centred * lax.rsqrt(spread + 1e-06) * (1.0 + scale_row) + shift_row).astype(jnp.bfloat16)

def width_norm(values, gain_vec):
    row_count = values.shape[0]
    square = lax.optimization_barrier(jnp.mean(values * values, axis=-1, keepdims=True))
    normed = (values * lax.rsqrt(square + 1e-06) * gain_vec).astype(jnp.bfloat16)
    return normed.reshape(row_count, values.shape[1] // HD, HD)

def reference(states, timesteps, lengths, modulation, w_query, w_key, w_value, w_out, q_gain, k_gain):
    scaling = 1.0 / math.sqrt(HD)
    group_width = HEADS * HD // N_HEAD
    positions = jnp.arange(SEQ, dtype=jnp.int32)

    def one_pair(pair_index):
        step_at = pair_index // PROMPTS
        prompt_at = pair_index % PROMPTS
        current = states[step_at, prompt_at]
        mod_rows = modulation[step_at]
        modulated = normed_rows(current, mod_rows[0], mod_rows[1])
        queries = width_norm(jnp.dot(modulated, w_query, preferred_element_type=jnp.float32), q_gain)
        keys_normed = width_norm(jnp.dot(modulated, w_key, preferred_element_type=jnp.float32), k_gain)
        value_rows = jnp.dot(modulated, w_value, preferred_element_type=jnp.float32).astype(jnp.bfloat16)
        value_rows = value_rows.reshape(SEQ, HEADS, HD)
        valid_keys = positions < lengths[prompt_at]

        def one_head(triple):
            query_head, key_head, value_head = triple
            scores = jnp.dot(query_head, key_head.T, preferred_element_type=jnp.float32) * scaling
            scores = jnp.where(valid_keys[None, :], scores, -jnp.inf)
            highest = lax.optimization_barrier(jnp.max(scores, axis=-1, keepdims=True))
            raised = jnp.exp(scores - highest)
            soft_rows = (raised / lax.optimization_barrier(jnp.sum(raised, axis=-1, keepdims=True))).astype(jnp.bfloat16)
            return jnp.dot(soft_rows, value_head, preferred_element_type=jnp.float32).astype(jnp.bfloat16)
        heads_out = lax.map(one_head, (queries.transpose(1, 0, 2), keys_normed.transpose(1, 0, 2), value_rows.transpose(1, 0, 2)))
        attended = heads_out.transpose(1, 0, 2).reshape(SEQ, HEADS * HD)
        projected = jnp.zeros((SEQ, D), jnp.float32)
        for group_at in range(N_HEAD):
            part_sum = jnp.dot(attended[:, group_at * group_width:(group_at + 1) * group_width], w_out[group_at * group_width:(group_at + 1) * group_width], preferred_element_type=jnp.float32)
            projected = projected + lax.optimization_barrier(part_sum.astype(jnp.bfloat16)).astype(jnp.float32)
        branch = mod_rows[2] * projected
        step_width = (timesteps[step_at, 1] - timesteps[step_at, 0]).astype(jnp.float32) / 1000.0
        return (branch.astype(jnp.bfloat16), step_width * (current + branch))
    updates, drifts = lax.map(one_pair, jnp.arange(STEPS * PROMPTS, dtype=jnp.int32))
    updates = updates.reshape(STEPS, PROMPTS, SEQ, D)
    drifts = drifts.reshape(STEPS, PROMPTS, SEQ, D)
    next_states = states[0][None] + jnp.cumsum(drifts, axis=0)
    return (next_states, updates)
```

```python
import math

import jax
import jax.numpy as jnp
from jax import lax
from jax.experimental import pallas as pl
from jax.experimental.pallas import tpu as pltpu
from jax.sharding import PartitionSpec as P

HD = 128
BF16 = jnp.bfloat16
F32 = jnp.float32
MESH = pl.DeviceIdType.MESH
NJ = 8
CW = 640
TOK = 128
LOCAL = 384
DEPTH = 320
HALF = 160
QUART = 80


class Link:
    def __init__(self, send, recv):
        self.send, self.recv, self.used = send, recv, 0

    def take(self, n=1):
        first = self.used
        self.used += n
        return first

    def copy(self, src, dst, sem, to):
        return pltpu.make_async_remote_copy(
            src_ref=src,
            dst_ref=dst,
            send_sem=self.send.at[sem],
            recv_sem=self.recv.at[sem],
            device_id=to,
            device_id_type=MESH,
        )


class Place:
    def __init__(self):
        step, head, fsdp = (lax.axis_index(a) for a in ("step", "head", "fsdp"))
        self.step, self.head = step, head
        self.y, self.x_lo, self.x_hi = step // 2, step % 2, fsdp
        self.x = self.x_hi * 2 + self.x_lo
        self.z, self.core = head // 2, head % 2

    def at(self, dx=0, dy=0, dz=0, other_core=False):
        x, y, z = (self.x + dx) % 4, (self.y + dy) % 4, (self.z + dz) % 4
        core = 1 - self.core if other_core else self.core
        return (y * 2 + x % 2, z * 2 + core, x // 2)

    def column(self, dx):
        x = (self.x + dx) % 4
        return (x % 2) * 2 + x // 2

    def row(self, dy):
        return (self.y + dy) % 4


class PlaneGather:
    def __init__(self, link, place, own, full):
        self.link, self.me, self.own, self.full = link, place, own, full
        self.base = link.take(16)
        self.started = []

    def go(self, slot, src, dst, to):
        copy = self.link.copy(src, dst, self.base + slot, to)
        copy.start()
        self.started.append(copy)

    def got(self, slot, dst):
        self.link.copy(dst, dst, self.base + slot, self.me.at(dx=1)).wait_recv()

    def start1(self):
        me, g = self.me, self.full
        y, c = me.y, me.column(0)
        g[y, c, 0] = self.own[0:HALF, :]
        g[y, c, 1] = self.own[HALF:DEPTH, :]
        a, b = self.own.at[0:HALF], self.own.at[HALF:DEPTH]
        self.go(0, a, g.at[y, c, 0], me.at(dx=1))
        self.go(1, a, g.at[y, c, 0], me.at(dx=-1))
        self.go(2, b, g.at[y, c, 1], me.at(dy=1))
        self.go(3, b, g.at[y, c, 1], me.at(dy=-1))

    def start2(self):
        me, g = self.me, self.full
        y, c = me.y, me.column(0)
        left, right = me.column(-1), me.column(1)
        below, above = me.row(-1), me.row(1)
        self.got(0, g.at[y, left, 0])
        part = g.at[y, left, 0, 0:QUART]
        self.go(4, part, part, me.at(dx=1))
        self.got(1, g.at[y, right, 0])
        part = g.at[y, right, 0, QUART:HALF]
        self.go(5, part, part, me.at(dx=-1))
        self.got(2, g.at[below, c, 1])
        part = g.at[below, c, 1, 0:QUART]
        self.go(6, part, part, me.at(dy=1))
        self.got(3, g.at[above, c, 1])
        part = g.at[above, c, 1, QUART:HALF]
        self.go(7, part, part, me.at(dy=-1))

    def start3(self):
        me, g = self.me, self.full
        y, c = me.y, me.column(0)
        far_x, far_y = me.column(2), me.row(2)
        self.got(4, g.at[y, far_x, 0, 0:QUART])
        self.got(5, g.at[y, far_x, 0, QUART:HALF])
        part = g.at[y, :, 0]
        self.go(8, part, part, me.at(dy=1))
        self.go(9, part, part, me.at(dy=-1))
        self.got(6, g.at[far_y, c, 1, 0:QUART])
        self.got(7, g.at[far_y, c, 1, QUART:HALF])
        part = g.at[:, c, 1]
        self.go(10, part, part, me.at(dx=1))
        self.go(11, part, part, me.at(dx=-1))

    def start4(self):
        me, g = self.me, self.full
        left, right = me.column(-1), me.column(1)
        below, above = me.row(-1), me.row(1)
        self.got(8, g.at[below, :, 0])
        part = g.at[below, :, 0, 0:QUART]
        self.go(12, part, part, me.at(dy=1))
        self.got(9, g.at[above, :, 0])
        part = g.at[above, :, 0, QUART:HALF]
        self.go(13, part, part, me.at(dy=-1))
        self.got(10, g.at[:, left, 1])
        part = g.at[:, left, 1, 0:QUART]
        self.go(14, part, part, me.at(dx=1))
        self.got(11, g.at[:, right, 1])
        part = g.at[:, right, 1, QUART:HALF]
        self.go(15, part, part, me.at(dx=-1))

    def finish(self):
        me, g = self.me, self.full
        far_x, far_y = me.column(2), me.row(2)
        self.got(12, g.at[far_y, :, 0, 0:QUART])
        self.got(13, g.at[far_y, :, 0, QUART:HALF])
        self.got(14, g.at[:, far_x, 1, 0:QUART])
        self.got(15, g.at[:, far_x, 1, QUART:HALF])
        for copy in self.started:
            copy.wait_send()


class TokenGather:
    def __init__(self, link, place, acts):
        self.link, self.me, self.acts = link, place, acts
        self.base = link.take(9)
        self.started = []

    def rows(self, dz, other=False, start=0, size=TOK):
        me = self.me
        z = (me.z + dz) % 4
        core = 1 - me.core if other else me.core
        return self.acts.at[pl.ds(pl.multiple_of((z * 2 + core) * TOK + start, 64), size), :]

    def go(self, slot, part, to):
        copy = self.link.copy(part, part, self.base + slot, to)
        copy.start()
        self.started.append(copy)

    def got(self, slot, part):
        self.link.copy(part, part, self.base + slot, self.me.at(dz=1)).wait_recv()

    def start1(self):
        me = self.me
        own = self.rows(0)
        self.go(0, own, me.at(dz=1))
        self.go(1, own, me.at(dz=-1))
        self.go(2, own, me.at(other_core=True))

    def start2(self):
        me = self.me
        self.got(0, self.rows(-1))
        self.go(3, self.rows(-1, size=64), me.at(dz=1))
        self.got(1, self.rows(1))
        self.go(4, self.rows(1, start=64, size=64), me.at(dz=-1))
        self.go(5, self.rows(-1), me.at(other_core=True))
        self.go(6, self.rows(1), me.at(other_core=True))

    def start3(self):
        me = self.me
        self.got(3, self.rows(2, size=64))
        self.go(7, self.rows(2, size=64), me.at(other_core=True))
        self.got(4, self.rows(2, start=64, size=64))
        self.go(8, self.rows(2, start=64, size=64), me.at(other_core=True))

    def finish(self):
        self.got(2, self.rows(0, other=True))
        self.got(5, self.rows(-1, other=True))
        self.got(6, self.rows(1, other=True))
        self.got(7, self.rows(2, other=True, size=64))
        self.got(8, self.rows(2, other=True, start=64, size=64))
        for copy in self.started:
            copy.wait_send()


def eye_mask():
    return lax.broadcasted_iota(jnp.int32, (128, 128), 0) == lax.broadcasted_iota(
        jnp.int32, (128, 128), 1
    )


def kernel(
    length_ref,
    width_ref,
    states_ref,
    mod_ref,
    gain_ref,
    wqk_ref,
    wv_ref,
    wo_ref,
    next_ref,
    update_ref,
    acts,
    qk_full,
    v_full,
    o_full,
    raw,
    qk,
    value,
    attended,
    squares,
    partial,
    summed,
    z_first,
    z_second,
    pair_out,
    pair_in,
    chain_out,
    chain_in,
    back_out,
    back_in,
    send_sem,
    recv_sem,
):
    me = Place()
    link = Link(send_sem, recv_sem)

    barrier = pltpu.get_barrier_semaphore()
    for d in range(1, 8):
        pl.semaphore_signal(
            barrier,
            inc=1,
            device_id=(me.step, (me.head + d) % 8, me.x_hi),
            device_id_type=MESH,
        )
    for to in (me.at(dx=1), me.at(dx=-1), me.at(dy=1), me.at(dy=-1)):
        pl.semaphore_signal(barrier, inc=1, device_id=to, device_id_type=MESH)
    pl.semaphore_wait(barrier, 11)

    w_qk = PlaneGather(link, me, wqk_ref, qk_full)
    w_v = PlaneGather(link, me, wv_ref, v_full)
    w_o = PlaneGather(link, me, wo_ref, o_full)
    tokens = TokenGather(link, me, acts)

    with jax.named_scope("norm"):
        w_qk.start1()
        shift, scale = mod_ref[0:1, :], 1.0 + mod_ref[1:2, :]

        @pl.loop(0, 8)
        def _(r):
            x = states_ref[pl.ds(r * 16, 16), :]
            centred = x - jnp.mean(x, axis=-1, keepdims=True)
            spread = jnp.mean(centred * centred, axis=-1, keepdims=True)
            y = centred * lax.rsqrt(spread + 1e-06) * scale + shift
            acts[pl.ds(pl.multiple_of(me.head * TOK + r * 16, 16), 16), :] = y.astype(BF16)

        tokens.start1()
    with jax.named_scope("qk_second"):
        w_qk.start2()
    with jax.named_scope("qk_third"):
        w_qk.start3()
        w_v.start1()
    with jax.named_scope("tokens_second"):
        tokens.start2()
    with jax.named_scope("qk_fourth"):
        w_qk.start4()
        w_v.start2()
    with jax.named_scope("tokens_third"):
        tokens.start3()
    with jax.named_scope("qk_finish"):
        w_qk.finish()
        w_v.start3()
        w_o.start1()
    with jax.named_scope("tokens_finish"):
        tokens.finish()

    with jax.named_scope("qk_matmul"):

        @pl.loop(0, 4)
        def _(m):
            rows = pl.ds(pl.multiple_of(m * 256, 256), 256)
            product = jnp.dot(
                acts[rows, :],
                qk_full[...].reshape(5120, 2 * LOCAL),
                preferred_element_type=F32,
            )
            raw[rows, :] = product
            for part in range(2):
                for b in range(2):
                    p = product[b * 128 : b * 128 + 128, part * LOCAL : (part + 1) * LOCAL]
                    total = jnp.sum(p * p, axis=1, keepdims=True)
                    row = jnp.sum(jnp.where(eye_mask(), total, 0.0), axis=0, keepdims=True)
                    squares[me.head, pl.ds(part * 8 + m * 2 + b, 1), :] = row

    with jax.named_scope("squares"):
        base = link.take(7)
        sent = []
        for d in range(1, 8):
            mine = squares.at[me.head]
            copy = link.copy(mine, mine, base + d - 1, (me.step, (me.head + d) % 8, me.x_hi))
            copy.start()
            sent.append(copy)
        w_v.start4()
        w_o.start2()
        for d in range(1, 8):
            theirs = squares.at[(me.head - d) % 8]
            link.copy(theirs, theirs, base + d - 1, (me.step, (me.head + d) % 8, me.x_hi)).wait_recv()
        for copy in sent:
            copy.wait_send()

    with jax.named_scope("qk_norm"):

        @pl.loop(0, 8)
        def _(b):
            rows = pl.ds(pl.multiple_of(b * 128, 128), 128)
            for part in range(2):
                total = squares[0, pl.ds(part * 8 + b, 1), :]
                for d in range(1, 8):
                    total = total + squares[d, pl.ds(part * 8 + b, 1), :]
                factor = lax.rsqrt(total / 3072.0 + 1e-06)
                column = jnp.sum(jnp.where(eye_mask(), factor, 0.0), axis=1, keepdims=True)
                cols = slice(part * LOCAL, (part + 1) * LOCAL)
                qk[rows, cols] = (raw[rows, cols] * column * gain_ref[part : part + 1, :]).astype(BF16)

    with jax.named_scope("v_finish"):
        w_v.finish()
        w_o.start3()

    with jax.named_scope("v_matmul"):

        @pl.loop(0, 4)
        def _(m):
            rows = pl.ds(pl.multiple_of(m * 256, 256), 256)
            product = jnp.dot(
                acts[rows, :], v_full[...].reshape(5120, LOCAL), preferred_element_type=F32
            )
            value[rows, :] = product.astype(BF16)

    with jax.named_scope("o_fourth"):
        w_o.start4()

    with jax.named_scope("attention"):
        length = length_ref[0]

        @pl.loop(0, 4)
        def _(m):
            rows = pl.ds(pl.multiple_of(m * 256, 256), 256)
            valid = lax.broadcasted_iota(jnp.int32, (256, 1024), 1) < length
            for h in range(3):
                q = qk[rows, h * HD : (h + 1) * HD]
                k = qk[:, LOCAL + h * HD : LOCAL + (h + 1) * HD]
                s = lax.dot_general(q, k, (((1,), (1,)), ((), ())), preferred_element_type=F32)
                s = jnp.where(valid, s * (1.0 / math.sqrt(HD)), -jnp.inf)
                e = jnp.exp(s - jnp.max(s, axis=-1, keepdims=True))
                p = (e * (1.0 / jnp.sum(e, axis=-1, keepdims=True))).astype(BF16)
                o = jnp.dot(p, value[:, h * HD : (h + 1) * HD], preferred_element_type=F32)
                attended[rows, h * HD : (h + 1) * HD] = o.astype(BF16)

    with jax.named_scope("o_finish"):
        w_o.finish()

    sib, first, second = link.take(NJ), link.take(2 * NJ), link.take(2 * NJ)
    pair, chain, back = link.take(NJ), link.take(NJ), link.take(NJ)
    up, down = me.at(dz=1), me.at(dz=-1)
    above, below, far = (me.z + 1) % 4, (me.z - 1) % 4, (me.z + 2) % 4
    partner = (me.y * 2 + 1 - me.x_lo, me.head, me.x_hi)
    y_up = me.at(dy=1)
    mine = pl.ds(pl.multiple_of(me.x_lo * 64, 64), 64)
    other = pl.ds(pl.multiple_of((1 - me.x_lo) * 64, 64), 64)
    width = width_ref[0]
    on_low = me.x_lo == 0

    def sib_copy(j):
        return link.copy(
            partial.at[j % 2, :, 1 - me.core], summed.at[j], sib + j, me.at(other_core=True)
        )

    def first_copies(j):
        return (
            link.copy(summed.at[j, far, 0:64], z_first.at[j, 0], first + 2 * j, up),
            link.copy(summed.at[j, far, 64:128], z_first.at[j, 1], first + 2 * j + 1, down),
        )

    def second_copies(j):
        return (
            link.copy(summed.at[j, above], z_second.at[j, 0], second + 2 * j, up),
            link.copy(summed.at[j, below], z_second.at[j, 1], second + 2 * j + 1, down),
        )

    def pair_copy(j):
        return link.copy(pair_out.at[j], pair_in.at[j], pair + j, partner)

    def chain_copy(j):
        return link.copy(chain_out.at[j], chain_in.at[j], chain + j, y_up)

    def back_copy(j):
        return link.copy(back_out.at[j], back_in.at[j], back + j, partner)

    def project(j):
        w = o_full[j // 2, pl.ds((j % 2) * 2, 2)].reshape(CW, LOCAL)
        for m in range(4):
            p = lax.dot_general(
                attended[m * 256 : (m + 1) * 256, :],
                w,
                (((1,), (1,)), ((), ())),
                preferred_element_type=F32,
            ).astype(BF16)
            partial[j % 2, m, 0] = p[0:128]
            partial[j % 2, m, 1] = p[128:256]
        sib_copy(j).start()

    def add_sibling(j):
        copy = sib_copy(j)
        copy.wait_recv()
        for m in range(4):
            own = partial[j % 2, m, me.core].astype(F32)
            summed[j, m] = (own + summed[j, m].astype(F32)).astype(BF16)
        copy.wait_send()
        for c in first_copies(j):
            c.start()

    def add_far(j):
        copies = first_copies(j)
        for c in copies:
            c.wait_recv()
        summed[j, above, 0:64] = (
            summed[j, above, 0:64].astype(F32) + z_first[j, 0].astype(F32)
        ).astype(BF16)
        summed[j, below, 64:128] = (
            summed[j, below, 64:128].astype(F32) + z_first[j, 1].astype(F32)
        ).astype(BF16)
        for c in second_copies(j):
            c.start()
        for c in copies:
            c.wait_send()

    def drift(j):
        copies = second_copies(j)
        for c in copies:
            c.wait_recv()
        cols = pl.ds(pl.multiple_of(j * CW, 128), CW)
        projected = (
            summed[j, me.z].astype(F32) + z_second[j, 0].astype(F32) + z_second[j, 1].astype(F32)
        )
        branch = mod_ref[2:3, cols] * projected
        update_ref[:, cols] = branch.astype(BF16)
        current = states_ref[:, cols]
        anchor = jnp.where(me.step == 0, current, 0.0)
        next_ref[:, cols] = width * (current + branch) + anchor
        pair_out[j] = next_ref[other, cols].astype(BF16)
        pair_copy(j).start()
        for c in copies:
            c.wait_send()

    def run_chain(j):
        cols = pl.ds(pl.multiple_of(j * CW, 128), CW)
        p_copy, c_copy = pair_copy(j), chain_copy(j)
        p_copy.wait_recv()
        received = pair_in[j].astype(F32)
        own = next_ref[mine, cols]

        @pl.when(me.y > 0)
        def _():
            c_copy.wait_recv()

        @pl.when(me.y == 0)
        def _():
            chain_in[j] = jnp.zeros((64, CW), BF16)

        earlier = chain_in[j].astype(F32)

        @pl.when(me.y < 3)
        def _():
            chain_out[j] = (earlier + own + received).astype(BF16)
            c_copy.start()

        back_out[j] = (earlier + jnp.where(on_low, own, 0.0)).astype(BF16)
        back_copy(j).start()
        next_ref[mine, cols] = own + (earlier + jnp.where(on_low, 0.0, received))
        p_copy.wait_send()

    def add_back(j):
        cols = pl.ds(pl.multiple_of(j * CW, 128), CW)
        copy = back_copy(j)
        copy.wait_recv()
        next_ref[other, cols] = next_ref[other, cols] + back_in[j].astype(F32)
        copy.wait_send()

        @pl.when(me.y < 3)
        def _():
            chain_copy(j).wait_send()

    with jax.named_scope("reduce"):
        stages = (project, add_sibling, add_far, drift, run_chain, add_back)

        @pl.loop(0, NJ + len(stages) - 1)
        def _(i):
            for lag, stage in enumerate(stages):
                j = i - lag

                @pl.when((j >= 0) & (j < NJ))
                def _(stage=stage, j=j):
                    stage(j)


def body(states, timesteps, lengths, modulation, w_query, w_key, w_value, w_out, q_gain, k_gain):
    width = (timesteps[0, 1] - timesteps[0, 0]).astype(F32) / 1000.0
    n_sems = 3 * 16 + 9 + 7 + 8 * NJ
    vmem = pl.BlockSpec(memory_space=pltpu.VMEM)
    smem = pl.BlockSpec(memory_space=pltpu.SMEM)
    nxt, update = pl.pallas_call(
        kernel,
        out_shape=(
            jax.ShapeDtypeStruct((TOK, 5120), F32),
            jax.ShapeDtypeStruct((TOK, 5120), BF16),
        ),
        in_specs=[smem, smem] + [vmem] * 6,
        out_specs=(vmem, vmem),
        scratch_shapes=[
            pltpu.VMEM((1024, 5120), BF16),
            pltpu.VMEM((4, 4, 2, HALF, 2 * LOCAL), BF16),
            pltpu.VMEM((4, 4, 2, HALF, LOCAL), BF16),
            pltpu.VMEM((4, 4, 2, HALF, LOCAL), BF16),
            pltpu.VMEM((1024, 2 * LOCAL), F32),
            pltpu.VMEM((1024, 2 * LOCAL), BF16),
            pltpu.VMEM((1024, LOCAL), BF16),
            pltpu.VMEM((1024, LOCAL), BF16),
            pltpu.VMEM((8, 16, 128), F32),
            pltpu.VMEM((2, 4, 2, TOK, CW), BF16),
            pltpu.VMEM((NJ, 4, TOK, CW), BF16),
            pltpu.VMEM((NJ, 2, 64, CW), BF16),
            pltpu.VMEM((NJ, 2, TOK, CW), BF16),
            pltpu.VMEM((NJ, 64, CW), BF16),
            pltpu.VMEM((NJ, 64, CW), BF16),
            pltpu.VMEM((NJ, 64, CW), BF16),
            pltpu.VMEM((NJ, 64, CW), BF16),
            pltpu.VMEM((NJ, 64, CW), BF16),
            pltpu.VMEM((NJ, 64, CW), BF16),
            pltpu.SemaphoreType.DMA((n_sems,)),
            pltpu.SemaphoreType.DMA((n_sems,)),
        ],
        compiler_params=pltpu.CompilerParams(
            collective_id=0,
            has_side_effects=True,
            vmem_limit_bytes=63 * 1024 * 1024,
        ),
    )(
        lengths,
        width.reshape(1),
        states[0, 0],
        modulation[0],
        jnp.stack([q_gain, k_gain]),
        jnp.concatenate([w_query, w_key], axis=1),
        w_value,
        w_out.T,
    )
    return (nxt[None, None], update[None, None])


def solution(mesh):
    in_specs = (
        P("step", "fsdp", "head", None),
        P("step", None),
        P("fsdp"),
        P("step", None, None),
        P(("step", "fsdp"), "head"),
        P(("step", "fsdp"), "head"),
        P(("step", "fsdp"), "head"),
        P("head", ("step", "fsdp")),
        P("head"),
        P("head"),
    )
    out_specs = (P("step", "fsdp", "head", None), P("step", "fsdp", "head", None))
    return jax.shard_map(body, mesh=mesh, in_specs=in_specs, out_specs=out_specs, check_vma=False)
```

```python
import math

import jax
import jax.numpy as jnp
from jax import lax
from jax.experimental import pallas as pl
from jax.experimental.pallas import tpu as pltpu
from jax.sharding import PartitionSpec as P

HD = 128
BF16 = jnp.bfloat16
F32 = jnp.float32
MESH = pl.DeviceIdType.MESH
TOK = 128
LOCAL = 384
PIECES = 5
NJ = 20
CW = 256
LAGS = (0, 1, 3, 5, 7, 9, 11)
SLOTS = 2
FLIGHT = 4


class Link:
    def __init__(self, send, recv):
        self.send, self.recv, self.used = send, recv, 0

    def take(self, n=1):
        first = self.used
        self.used += n
        return first

    def copy(self, src, dst, sem, to, send_sem=None):
        return pltpu.make_async_remote_copy(
            src_ref=src,
            dst_ref=dst,
            send_sem=self.send.at[sem if send_sem is None else send_sem],
            recv_sem=self.recv.at[sem],
            device_id=to,
            device_id_type=MESH,
        )


class Place:
    def __init__(self):
        step, head, fsdp = (lax.axis_index(a) for a in ("step", "head", "fsdp"))
        self.step, self.head = step, head
        self.y, self.x_lo, self.x_hi = step // 2, step % 2, fsdp
        self.x = self.x_hi * 2 + self.x_lo
        self.z, self.core = head // 2, head % 2

    def at(self, dx=0, dy=0, dz=0, other_core=False):
        x, y, z = (self.x + dx) % 4, (self.y + dy) % 4, (self.z + dz) % 4
        core = 1 - self.core if other_core else self.core
        return (y * 2 + x % 2, z * 2 + core, x // 2)

    def column(self, dx):
        x = (self.x + dx) % 4
        return (x % 2) * 2 + x // 2

    def row(self, dy):
        return (self.y + dy) % 4


class PlaneGather:
    def __init__(self, link, place, view, half):
        me = place
        whole, low, high = slice(0, half), slice(0, half // 2), slice(half // 2, half)
        every = slice(0, 4)
        y, c = me.y, me.column(0)
        left, right, far_x = me.column(-1), me.column(1), me.column(2)
        below, above, far_y = me.row(-1), me.row(1), me.row(2)
        east, west, north, south = me.at(dx=1), me.at(dx=-1), me.at(dy=1), me.at(dy=-1)
        self.link, self.view, self.base = link, view, link.take(16)
        self.sends = (
            ((y, c, 0, whole), east),
            ((y, c, 0, whole), west),
            ((y, c, 1, whole), north),
            ((y, c, 1, whole), south),
            ((y, left, 0, low), east),
            ((y, right, 0, high), west),
            ((below, c, 1, low), north),
            ((above, c, 1, high), south),
            ((y, every, 0, whole), north),
            ((y, every, 0, whole), south),
            ((every, c, 1, whole), east),
            ((every, c, 1, whole), west),
            ((below, every, 0, low), north),
            ((above, every, 0, high), south),
            ((every, left, 1, low), east),
            ((every, right, 1, high), west),
        )
        self.receives = (
            (y, left, 0, whole),
            (y, right, 0, whole),
            (below, c, 1, whole),
            (above, c, 1, whole),
            (y, far_x, 0, low),
            (y, far_x, 0, high),
            (far_y, c, 1, low),
            (far_y, c, 1, high),
            (below, every, 0, whole),
            (above, every, 0, whole),
            (every, left, 1, whole),
            (every, right, 1, whole),
            (far_y, every, 0, low),
            (far_y, every, 0, high),
            (every, far_x, 1, low),
            (every, far_x, 1, high),
        )

    def copy(self, slot, args):
        part = self.view(*args)
        return self.link.copy(part, part, self.base + slot, self.sends[slot][1])

    def start(self, *slots):
        for slot in slots:
            self.copy(slot, self.sends[slot][0]).start()

    def got(self, *slots):
        for slot in slots:
            self.copy(slot, self.receives[slot]).wait_recv()

    def start1(self):
        self.start(0, 1, 2, 3)

    def start2(self):
        for slot in range(4):
            self.got(slot)
            self.start(slot + 4)

    def start3(self):
        self.got(4, 5)
        self.start(8, 9)
        self.got(6, 7)
        self.start(10, 11)

    def start4(self):
        for slot in range(8, 12):
            self.got(slot)
            self.start(slot + 4)

    def finish(self):
        self.got(12, 13, 14, 15)

    def drain(self):
        for slot in range(16):
            self.copy(slot, self.sends[slot][0]).wait_send()


class TokenGather:
    def __init__(self, link, place, acts):
        self.link, self.me, self.acts = link, place, acts
        self.base = link.take(9)
        self.started = []

    def rows(self, dz, other=False, start=0, size=TOK):
        me = self.me
        z = (me.z + dz) % 4
        core = 1 - me.core if other else me.core
        return self.acts.at[pl.ds(pl.multiple_of((z * 2 + core) * TOK + start, 64), size), :]

    def go(self, slot, part, to):
        copy = self.link.copy(part, part, self.base + slot, to)
        copy.start()
        self.started.append(copy)

    def got(self, slot, part):
        self.link.copy(part, part, self.base + slot, self.me.at(dz=1)).wait_recv()

    def start1(self):
        me = self.me
        own = self.rows(0)
        self.go(0, own, me.at(dz=1))
        self.go(1, own, me.at(dz=-1))
        self.go(2, own, me.at(other_core=True))

    def start2(self):
        me = self.me
        self.got(0, self.rows(-1))
        self.go(3, self.rows(-1, size=64), me.at(dz=1))
        self.got(1, self.rows(1))
        self.go(4, self.rows(1, start=64, size=64), me.at(dz=-1))
        self.go(5, self.rows(-1), me.at(other_core=True))
        self.go(6, self.rows(1), me.at(other_core=True))

    def start3(self):
        me = self.me
        self.got(3, self.rows(2, size=64))
        self.go(7, self.rows(2, size=64), me.at(other_core=True))
        self.got(4, self.rows(2, start=64, size=64))
        self.go(8, self.rows(2, start=64, size=64), me.at(other_core=True))

    def own_chip(self):
        self.got(2, self.rows(0, other=True))

    def near_chips(self):
        self.got(5, self.rows(-1, other=True))
        self.got(6, self.rows(1, other=True))

    def far_chip(self):
        self.got(7, self.rows(2, other=True, size=64))
        self.got(8, self.rows(2, other=True, start=64, size=64))

    def drain(self):
        for copy in self.started:
            copy.wait_send()


def eye_mask():
    return lax.broadcasted_iota(jnp.int32, (128, 128), 0) == lax.broadcasted_iota(
        jnp.int32, (128, 128), 1
    )


def kernel(
    length_ref,
    time_ref,
    q_gain_ref,
    k_gain_ref,
    states_hbm,
    mod_hbm,
    wq_hbm,
    wk_hbm,
    wv_hbm,
    wo_hbm,
    next_ref,
    update_ref,
    states,
    mod,
    acts,
    w_a,
    w_b,
    w_c,
    w_d,
    w_e,
    o_full,
    raw,
    qk,
    value,
    probs,
    attended,
    squares,
    partial,
    summed,
    z_first,
    z_second,
    pair_out,
    pair_in,
    chain_out,
    chain_in,
    back_out,
    back_in,
    send_sem,
    recv_sem,
    local_sem,
):
    me = Place()
    link = Link(send_sem, recv_sem)

    barrier = pltpu.get_barrier_semaphore()
    for d in range(1, 8):
        pl.semaphore_signal(
            barrier,
            inc=1,
            device_id=(me.step, (me.head + d) % 8, me.x_hi),
            device_id_type=MESH,
        )
    for to in (me.at(dx=1), me.at(dx=-1), me.at(dy=1), me.at(dy=2), me.at(dy=3)):
        pl.semaphore_signal(barrier, inc=1, device_id=to, device_id_type=MESH)

    y, c = me.y, me.column(0)
    local = []
    for src, dst in (
        (wq_hbm.at[:, :, 0:256], w_a.at[y, c]),
        (states_hbm.at[0, 0], states),
        (mod_hbm, mod),
        (wq_hbm.at[:, :, 256:384], w_b.at[y, c, :, :, 0:128]),
        (wk_hbm.at[:, :, 0:128], w_b.at[y, c, :, :, 128:256]),
        (wk_hbm.at[:, :, 128:384], w_c.at[y, c]),
        (wv_hbm.at[:, :, 0:256], w_d.at[y, c]),
        (wv_hbm.at[:, :, 256:384], w_e.at[y, c]),
        (wo_hbm, o_full.at[:, y, c]),
    ):
        copy = pltpu.make_async_copy(src, dst, local_sem.at[len(local)])
        copy.start()
        local.append(copy)
    local[0].wait()
    pl.semaphore_wait(barrier, 12)

    def weight(full):
        return PlaneGather(link, me, lambda y, c, h, r: full.at[y, c, h, r], 160)

    def out_weight(first, last):
        return PlaneGather(link, me, lambda y, c, h, r: o_full.at[first:last, y, c, h, r], 32)

    g_a, g_b, g_c, g_d, g_e = (weight(w) for w in (w_a, w_b, w_c, w_d, w_e))
    o_a, o_b, o_c = out_weight(0, 1), out_weight(1, 2), out_weight(2, 5)
    tokens = TokenGather(link, me, acts)

    def product(rows, w):
        return jnp.dot(acts[rows, :], w[...].reshape(5120, w.shape[-1]), preferred_element_type=F32)

    def raw_product(dz, w, column):
        rows = pl.ds(pl.multiple_of(((me.z + dz) % 4) * 256, 256), 256)
        raw[rows, column * 256 : column * 256 + 256] = product(rows, w)

    with jax.named_scope("norm"):
        g_a.start1()
        for copy in local[1:]:
            copy.wait()
        g_b.start1()
        shift, scale = mod[0], 1.0 + mod[1]

        @pl.loop(0, 8)
        def _(r):
            x = states[pl.ds(pl.multiple_of(r * 16, 16), 16), :]
            centred = x - jnp.mean(x, axis=-1, keepdims=True)
            spread = jnp.mean(centred * centred, axis=-1, keepdims=True)
            out = centred * lax.rsqrt(spread + 1e-06) * scale + shift
            acts[pl.ds(pl.multiple_of(me.head * TOK + r * 16, 16), 16), :] = out.astype(BF16)

        tokens.start1()
    with jax.named_scope("a2"):
        g_a.start2()
        g_c.start1()
    with jax.named_scope("b2"):
        g_b.start2()
    with jax.named_scope("a3"):
        g_a.start3()
        g_c.start2()
    with jax.named_scope("a4"):
        g_a.start4()
        g_b.start3()
        g_d.start1()
    with jax.named_scope("a5"):
        g_a.finish()
        g_c.start3()
        g_d.start2()
        tokens.own_chip()
    with jax.named_scope("own_a"):
        raw_product(0, w_a, 0)
    with jax.named_scope("b4"):
        g_b.start4()
        g_e.start1()
    with jax.named_scope("tokens2"):
        tokens.start2()
    with jax.named_scope("b5"):
        g_b.finish()
        g_d.start3()
        g_e.start2()
    with jax.named_scope("own_b"):
        raw_product(0, w_b, 1)
    with jax.named_scope("c4"):
        g_c.start4()
        o_a.start1()
    with jax.named_scope("near_wait"):
        tokens.near_chips()
    with jax.named_scope("near_ab"):

        @pl.loop(0, 2)
        def _(i):
            raw_product(2 * i + 3, w_a, 0)
            raw_product(2 * i + 3, w_b, 1)

    with jax.named_scope("c5"):
        g_c.finish()
        g_e.start3()
        o_a.start2()
    with jax.named_scope("near_c"):

        @pl.loop(0, 3)
        def _(i):
            raw_product(i + 3, w_c, 2)

    with jax.named_scope("d4"):
        g_d.start4()
        o_b.start1()
    with jax.named_scope("tokens3"):
        tokens.start3()
    with jax.named_scope("tokens4"):
        tokens.far_chip()
    with jax.named_scope("far"):
        raw_product(2, w_a, 0)
        raw_product(2, w_b, 1)
        raw_product(2, w_c, 2)
    with jax.named_scope("squares"):

        @pl.loop(0, 8)
        def _(b):
            rows = pl.ds(pl.multiple_of(b * 128, 128), 128)
            for part in range(2):
                p = raw[rows, part * LOCAL : (part + 1) * LOCAL]
                total = jnp.sum(p * p, axis=1, keepdims=True)
                row = jnp.sum(jnp.where(eye_mask(), total, 0.0), axis=0, keepdims=True)
                squares[me.head, pl.ds(part * 8 + b, 1), :] = row

        base = link.take(7)
        sent = []
        for d in range(1, 8):
            own = squares.at[me.head]
            copy = link.copy(own, own, base + d - 1, (me.step, (me.head + d) % 8, me.x_hi))
            copy.start()
            sent.append(copy)
    length = length_ref[0]

    def softmax(h, m):
        rows = pl.ds(pl.multiple_of(m * 256, 256), 256)
        valid = lax.broadcasted_iota(jnp.int32, (256, 1024), 1) < length
        q = qk[rows, h * HD : (h + 1) * HD]
        k = qk[:, LOCAL + h * HD : LOCAL + (h + 1) * HD]
        s = lax.dot_general(q, k, (((1,), (1,)), ((), ())), preferred_element_type=F32)
        s = jnp.where(valid, s * (math.log2(math.e) / math.sqrt(HD)), -jnp.inf)
        e = jnp.exp2(s - jnp.max(s, axis=-1, keepdims=True))
        probs[h, rows, :] = (e * (1.0 / jnp.sum(e, axis=-1, keepdims=True))).astype(BF16)

    def attend(h, m):
        rows = pl.ds(pl.multiple_of(m * 256, 256), 256)
        o = jnp.dot(probs[h, rows, :], value[:, h * HD : (h + 1) * HD], preferred_element_type=F32)
        attended[rows, h * HD : (h + 1) * HD] = o.astype(BF16)

    def value_product(w, cols, m):
        rows = pl.ds(pl.multiple_of(m * 256, 256), 256)
        value[rows, cols] = product(rows, w).astype(BF16)

    with jax.named_scope("e4"):
        g_e.start4()
        o_a.start3()
        o_b.start2()
    with jax.named_scope("d5"):
        g_d.finish()
        o_c.start1()
    with jax.named_scope("value_d"):

        @pl.loop(0, 4)
        def _(m):
            value_product(w_d, slice(0, 256), m)

    with jax.named_scope("squares_wait"):
        for d in range(1, 8):
            theirs = squares.at[(me.head - d) % 8]
            link.copy(theirs, theirs, base + d - 1, (me.step, (me.head + d) % 8, me.x_hi)).wait_recv()
        for copy in sent:
            copy.wait_send()

    with jax.named_scope("qk_norm"):

        @pl.loop(0, 8)
        def _(b):
            rows = pl.ds(pl.multiple_of(b * 128, 128), 128)
            for part, gain in enumerate((q_gain_ref, k_gain_ref)):
                total = squares[0, pl.ds(part * 8 + b, 1), :]
                for d in range(1, 8):
                    total = total + squares[d, pl.ds(part * 8 + b, 1), :]
                factor = lax.rsqrt(total / 3072.0 + 1e-06)
                column = jnp.sum(jnp.where(eye_mask(), factor, 0.0), axis=1, keepdims=True)
                cols = slice(part * LOCAL, (part + 1) * LOCAL)
                qk[rows, cols] = (raw[rows, cols] * column * gain[...].reshape(1, LOCAL)).astype(BF16)

    with jax.named_scope("softmax0"):

        @pl.loop(0, 4)
        def _(m):
            softmax(0, m)

    with jax.named_scope("o_a4"):
        o_a.start4()
        o_b.start3()
        o_c.start2()
    with jax.named_scope("e5"):
        g_e.finish()
    with jax.named_scope("softmax1_value_e"):

        @pl.loop(0, 4)
        def _(m):
            softmax(1, m)
            value_product(w_e, slice(256, 384), m)

    with jax.named_scope("o_b4"):
        o_b.start4()
        o_c.start3()
    with jax.named_scope("softmax2_attend0"):

        @pl.loop(0, 4)
        def _(m):
            softmax(2, m)
            attend(0, m)

    with jax.named_scope("attend12"):

        @pl.loop(0, 4)
        def _(m):
            attend(1, m)
            attend(2, m)

    with jax.named_scope("o_a5"):
        o_a.finish()
        for g in (g_a, g_b, g_c, g_d, g_e, tokens):
            g.drain()

    sending = link.used
    sib, first, second = link.take(NJ), link.take(2 * NJ), link.take(2 * NJ)
    pair, chain, back = link.take(NJ), link.take(3 * NJ), link.take(NJ)
    up, down = me.at(dz=1), me.at(dz=-1)
    above, below, far = (me.z + 1) % 4, (me.z - 1) % 4, (me.z + 2) % 4
    partner = (me.y * 2 + 1 - me.x_lo, me.head, me.x_hi)
    later = [me.at(dy=d) for d in (1, 2, 3)]
    on_low = me.x_lo == 0
    lower = lax.broadcasted_iota(jnp.int32, (TOK, 128), 1) < 64
    width = (jnp.full((1, 128), time_ref[0, 1] - time_ref[0, 0], jnp.int32)).astype(F32) / 1000.0

    def turn(j, kind):
        return sending + kind * FLIGHT + j % FLIGHT

    def sib_copy(j):
        return link.copy(
            partial.at[j % SLOTS, :, 1 - me.core], summed.at[j], sib + j, me.at(other_core=True), turn(j, 0)
        )

    def first_copies(j):
        return (
            link.copy(summed.at[j, far, 0:64], z_first.at[j, 0], first + 2 * j, up, turn(j, 1)),
            link.copy(summed.at[j, far, 64:128], z_first.at[j, 1], first + 2 * j + 1, down, turn(j, 2)),
        )

    def second_copies(j):
        return (
            link.copy(summed.at[j, above], z_second.at[j, 0], second + 2 * j, up, turn(j, 3)),
            link.copy(summed.at[j, below], z_second.at[j, 1], second + 2 * j + 1, down, turn(j, 4)),
        )

    def pair_copy(j):
        return link.copy(pair_out.at[j], pair_in.at[j], pair + j, partner, turn(j, 5))

    def chain_copy(j, d):
        return link.copy(
            chain_out.at[j], chain_in.at[j, d - 1], chain + 3 * j + d - 1, later[d - 1], turn(j, 6 + d)
        )

    def back_copy(j):
        return link.copy(back_out.at[j], back_in.at[j], back + j, partner, turn(j, 6))

    def natural(j, m):
        piece, tile = j // 4, (j % 4) * 2 + m
        odd = piece % 2
        low = 5 * tile + (piece + 5 * odd) // 2
        high = 5 * tile + 2 * (1 - odd) + (piece - odd) // 2
        return (
            pl.ds(pl.multiple_of(low * 128, 128), 128),
            pl.ds(pl.multiple_of(high * 128, 128), 128),
        )

    def kept(j, half):
        start = (j % 8) * 128 + half * 64
        return pl.ds(pl.multiple_of(start, 64), 64), pl.ds(pl.multiple_of((j // 8) * 256, 256), 256)

    def project(j):
        w = o_full[j // 4, j % 4].reshape(CW, LOCAL)
        for m in range(4):
            p = lax.dot_general(
                attended[m * 256 : (m + 1) * 256, :],
                w,
                (((1,), (1,)), ((), ())),
                preferred_element_type=F32,
            ).astype(BF16)
            partial[j % SLOTS, m, 0] = p[0:128]
            partial[j % SLOTS, m, 1] = p[128:256]
        sib_copy(j).start()

    def add_sibling(j):
        copy = sib_copy(j)
        copy.wait_recv()
        for m in range(4):
            own = partial[j % SLOTS, m, me.core].astype(F32)
            summed[j, m] = (own + summed[j, m].astype(F32)).astype(BF16)
        copy.wait_send()
        for c in first_copies(j):
            c.start()

    def add_far(j):
        copies = first_copies(j)
        for c in copies:
            c.wait_recv()
        summed[j, above, 0:64] = (
            summed[j, above, 0:64].astype(F32) + z_first[j, 0].astype(F32)
        ).astype(BF16)
        summed[j, below, 64:128] = (
            summed[j, below, 64:128].astype(F32) + z_first[j, 1].astype(F32)
        ).astype(BF16)
        for c in second_copies(j):
            c.start()
        for c in copies:
            c.wait_send()

    def drift(j):
        copies = second_copies(j)
        for c in copies:
            c.wait_recv()
        rows = pl.ds(pl.multiple_of((j % 8) * 128, 128), 128)
        for m in range(2):
            lanes = slice(m * 128, (m + 1) * 128)
            total = (
                summed[j, me.z, :, lanes].astype(F32)
                + z_second[j, 0, :, lanes].astype(F32)
                + z_second[j, 1, :, lanes].astype(F32)
            )
            projected = jnp.where((j // 4) % 2 == 1, pltpu.roll(total, 64, 1), total)
            low, high = natural(j, m)
            gate = jnp.where(lower[0:1], mod[2, :, low], mod[2, :, high])
            branch = gate * projected
            update_ref[:, low] = jnp.where(lower, branch, update_ref[:, low].astype(F32)).astype(BF16)
            update_ref[:, high] = jnp.where(lower, update_ref[:, high].astype(F32), branch).astype(BF16)
            current = jnp.where(lower, states[:, low], states[:, high])
            anchor = jnp.where(me.step == 0, current, 0.0)
            raw[rows, pl.ds(pl.multiple_of((j // 8) * 256 + m * 128, 128), 128)] = (
                width * (current + branch) + anchor
            )
        pair_out[j] = raw[kept(j, 1 - me.x_lo)].astype(BF16)
        pair_copy(j).start()
        for c in copies:
            c.wait_send()

    def add_pair(j):
        copy = pair_copy(j)
        copy.wait_recv()
        chain_out[j] = (raw[kept(j, me.x_lo)] + pair_in[j].astype(F32)).astype(BF16)
        for d in (1, 2, 3):

            @pl.when(me.y + d < 4)
            def _(d=d):
                chain_copy(j, d).start()

        copy.wait_send()

    def add_earlier(j):
        for d in (1, 2, 3):

            @pl.when(me.y >= d)
            def _(d=d):
                chain_copy(j, d).wait_recv()

        earlier = jnp.zeros((64, CW), F32)
        for d in (1, 2, 3):
            earlier = earlier + jnp.where(me.y >= d, chain_in[j, d - 1].astype(F32), 0.0)
        mine = kept(j, me.x_lo)
        own = raw[mine]
        back_out[j] = (earlier + jnp.where(on_low, own, 0.0)).astype(BF16)
        back_copy(j).start()
        raw[mine] = own + (earlier + jnp.where(on_low, 0.0, pair_in[j].astype(F32)))
        for d in (1, 2, 3):

            @pl.when(me.y + d < 4)
            def _(d=d):
                chain_copy(j, d).wait_send()

    def add_back(j):
        copy = back_copy(j)
        copy.wait_recv()
        other = kept(j, 1 - me.x_lo)
        raw[other] = raw[other] + back_in[j].astype(F32)
        rows = pl.ds(pl.multiple_of((j % 8) * 128, 128), 128)
        for m in range(2):
            low, high = natural(j, m)
            total = raw[rows, pl.ds(pl.multiple_of((j // 8) * 256 + m * 128, 128), 128)]
            next_ref[:, low] = jnp.where(lower, total, next_ref[:, low])
            next_ref[:, high] = jnp.where(lower, next_ref[:, high], total)
        copy.wait_send()

    with jax.named_scope("reduce"):
        stages = (project, add_sibling, add_far, drift, add_pair, add_earlier, add_back)

        @pl.loop(0, NJ + LAGS[-1])
        def _(i):
            @pl.when(i == 2)
            def _():
                o_c.start4()

            @pl.when(i == 4)
            def _():
                o_b.finish()

            @pl.when(i == 8)
            def _():
                o_c.finish()

            for lag, stage in zip(LAGS, stages):
                j = i - lag

                @pl.when((j >= 0) & (j < NJ))
                def _(stage=stage, j=j):
                    stage(j)

    for g in (o_a, o_b, o_c):
        g.drain()


def body(states, timesteps, lengths, modulation, w_query, w_key, w_value, w_out, q_gain, k_gain):
    n_gather = 8 * 16 + 9 + 7
    vmem = pl.BlockSpec(memory_space=pltpu.VMEM)
    smem = pl.BlockSpec(memory_space=pltpu.SMEM)
    anywhere = pl.BlockSpec(memory_space=pl.ANY)
    nxt, update = pl.pallas_call(
        kernel,
        out_shape=(
            jax.ShapeDtypeStruct((TOK, 5120), F32),
            jax.ShapeDtypeStruct((TOK, 5120), BF16),
        ),
        in_specs=[smem, smem, vmem, vmem] + [anywhere] * 6,
        out_specs=(vmem, vmem),
        scratch_shapes=[
            pltpu.VMEM((TOK, 5120), F32),
            pltpu.VMEM((3, 1, 5120), F32),
            pltpu.VMEM((1024, 5120), BF16),
            pltpu.VMEM((4, 4, 2, 160, 256), BF16),
            pltpu.VMEM((4, 4, 2, 160, 256), BF16),
            pltpu.VMEM((4, 4, 2, 160, 256), BF16),
            pltpu.VMEM((4, 4, 2, 160, 256), BF16),
            pltpu.VMEM((4, 4, 2, 160, 128), BF16),
            pltpu.VMEM((PIECES, 4, 4, 2, 32, LOCAL), BF16),
            pltpu.VMEM((1024, 2 * LOCAL), F32),
            pltpu.VMEM((1024, 2 * LOCAL), BF16),
            pltpu.VMEM((1024, LOCAL), BF16),
            pltpu.VMEM((3, 1024, 1024), BF16),
            pltpu.VMEM((1024, LOCAL), BF16),
            pltpu.VMEM((8, 16, 128), F32),
            pltpu.VMEM((SLOTS, 4, 2, TOK, CW), BF16),
            pltpu.VMEM((NJ, 4, TOK, CW), BF16),
            pltpu.VMEM((NJ, 2, 64, CW), BF16),
            pltpu.VMEM((NJ, 2, TOK, CW), BF16),
            pltpu.VMEM((NJ, 64, CW), BF16),
            pltpu.VMEM((NJ, 64, CW), BF16),
            pltpu.VMEM((NJ, 64, CW), BF16),
            pltpu.VMEM((NJ, 3, 64, CW), BF16),
            pltpu.VMEM((NJ, 64, CW), BF16),
            pltpu.VMEM((NJ, 64, CW), BF16),
            pltpu.SemaphoreType.DMA((n_gather + 10 * FLIGHT,)),
            pltpu.SemaphoreType.DMA((n_gather + 10 * NJ,)),
            pltpu.SemaphoreType.DMA((9,)),
        ],
        compiler_params=pltpu.CompilerParams(
            collective_id=0,
            has_side_effects=True,
            vmem_limit_bytes=63 * 1024 * 1024,
        ),
    )(
        lengths,
        timesteps,
        q_gain,
        k_gain,
        states,
        modulation.transpose(1, 0, 2),
        w_query.reshape(2, 160, LOCAL),
        w_key.reshape(2, 160, LOCAL),
        w_value.reshape(2, 160, LOCAL),
        w_out.T.reshape(PIECES, 2, 32, LOCAL),
    )
    return (nxt[None, None], update[None, None])


def solution(mesh):
    in_specs = (
        P("step", "fsdp", "head", None),
        P("step", None),
        P("fsdp"),
        P("step", None, None),
        P(("step", "fsdp"), "head"),
        P(("step", "fsdp"), "head"),
        P(("step", "fsdp"), "head"),
        P("head", ("step", "fsdp")),
        P("head"),
        P("head"),
    )
    out_specs = (P("step", "fsdp", "head", None), P("step", "fsdp", "head", None))
    return jax.shard_map(body, mesh=mesh, in_specs=in_specs, out_specs=out_specs, check_vma=False)
```

```python
import math

import jax
import jax.numpy as jnp
from jax import lax
from jax.experimental import pallas as pl
from jax.experimental.pallas import tpu as pltpu
from jax.sharding import PartitionSpec as P

HD = 128
BF16 = jnp.bfloat16
F32 = jnp.float32
MESH = pl.DeviceIdType.MESH
TOK = 128
LOCAL = 384
PIECES = 5
NJ = 20
CW = 256
LAGS = (0, 1, 3, 5, 7, 9, 11)
SLOTS = 2
FLIGHT = 4
AHEAD = 8


class Link:
    def __init__(self, send, recv, some_device):
        self.send, self.recv, self.to = send, recv, some_device
        self.sends, self.recvs = 0, 0

    def take(self, sends, recvs):
        first = self.sends, self.recvs
        self.sends, self.recvs = self.sends + sends, self.recvs + recvs
        return first

    def copy(self, src, dst, send, recv, to):
        return pltpu.make_async_remote_copy(
            src_ref=src,
            dst_ref=dst,
            send_sem=self.send.at[send],
            recv_sem=self.recv.at[recv],
            device_id=to,
            device_id_type=MESH,
        )

    def sent(self, send, size):
        self.copy(size, size, send, 0, self.to).wait_send()

    def got(self, recv, size):
        self.copy(size, size, 0, recv, self.to).wait_recv()


class Place:
    def __init__(self):
        step, head, fsdp = (lax.axis_index(a) for a in ("step", "head", "fsdp"))
        self.step, self.head = step, head
        self.y, self.x_lo, self.x_hi = step // 2, step % 2, fsdp
        self.x = self.x_hi * 2 + self.x_lo
        self.z, self.core = head // 2, head % 2

    def at(self, dx=0, dy=0, dz=0, other_core=False):
        x, y, z = (self.x + dx) % 4, (self.y + dy) % 4, (self.z + dz) % 4
        core = 1 - self.core if other_core else self.core
        return (y * 2 + x % 2, z * 2 + core, x // 2)

    def column(self, dx):
        x = (self.x + dx) % 4
        return (x % 2) * 2 + x // 2

    def row(self, dy):
        return (self.y + dy) % 4


class PlaneGather:
    def __init__(self, link, place, view, half):
        me = place
        whole, low, high = slice(0, half), slice(0, half // 2), slice(half // 2, half)
        every = slice(0, 4)
        y, c = me.y, me.column(0)
        left, right, far_x = me.column(-1), me.column(1), me.column(2)
        below, above, far_y = me.row(-1), me.row(1), me.row(2)
        east, west, north, south = me.at(dx=1), me.at(dx=-1), me.at(dy=1), me.at(dy=-1)
        self.link, self.view = link, view
        self.s, self.r = link.take(4, 6)
        self.sends = (
            ((y, c, 0, whole), east),
            ((y, c, 0, whole), west),
            ((y, c, 1, whole), north),
            ((y, c, 1, whole), south),
            ((y, left, 0, low), east),
            ((y, right, 0, high), west),
            ((below, c, 1, low), north),
            ((above, c, 1, high), south),
            ((y, every, 0, whole), north),
            ((y, every, 0, whole), south),
            ((every, c, 1, whole), east),
            ((every, c, 1, whole), west),
            ((below, every, 0, low), north),
            ((above, every, 0, high), south),
            ((every, left, 1, low), east),
            ((every, right, 1, high), west),
        )
        two = slice(0, 2)
        self.pair = view(y, two, 0, whole)
        self.rows = view(two, every, 0, whole)
        self.half = view(every, every, 0, whole)
        self.row = view(y, every, 0, whole)

    def start(self, first, last):
        for slot in range(first, last):
            args, to = self.sends[slot]
            part = self.view(*args)
            recv = (0, 0, 1, 1, 2, 2, 2, 2, 3, 3, 4, 4, 5, 5, 5, 5)[slot]
            self.link.copy(part, part, self.s + slot // 4, self.r + recv, to).start()

    def got(self, n, size):
        self.link.got(self.r + n, size)

    def start1(self):
        self.start(0, 4)

    def start2(self):
        self.got(0, self.pair)
        self.start(4, 6)
        self.got(1, self.pair)
        self.start(6, 8)

    def start3(self):
        self.got(2, self.pair)
        self.start(8, 12)

    def start4(self):
        self.got(3, self.rows)
        self.start(12, 14)
        self.got(4, self.rows)
        self.start(14, 16)

    def finish(self):
        self.got(5, self.rows)

    def drain(self):
        for phase, size in enumerate((self.row, self.pair, self.half, self.rows)):
            self.link.sent(self.s + phase, size)


class TokenGather:
    def __init__(self, link, place, acts):
        self.link, self.me, self.acts = link, place, acts
        self.s, self.r = link.take(6, 6)

    def rows(self, dz, start=0, size=TOK):
        me = self.me
        z = (me.z + dz) % 4
        return self.acts.at[pl.ds(pl.multiple_of((z * 2 + me.core) * TOK + start, 64), size), :]

    def low(self, dz):
        return self.rows(dz, 0, 64)

    def high(self, dz):
        return self.rows(dz, 64, 64)

    def go(self, n, part, to):
        self.link.copy(part, part, self.s + n, self.r + n, to).start()

    def got(self, n, rows=TOK):
        self.link.got(self.r + n, self.acts.at[0:rows])

    def start1(self):
        up, down = self.me.at(dz=1), self.me.at(dz=-1)
        self.go(0, self.low(0), up)
        self.go(0, self.high(0), down)
        self.go(1, self.high(0), up)
        self.go(1, self.low(0), down)
        self.go(2, self.rows(0), self.me.at(other_core=True))

    def start2(self):
        self.got(0)
        self.go(3, self.low(-1), self.me.at(dz=1))
        self.go(3, self.high(1), self.me.at(dz=-1))

    def start3(self):
        other = self.me.at(other_core=True)
        self.got(1)
        self.go(4, self.rows(-1), other)
        self.go(4, self.rows(1), other)

    def start4(self):
        self.got(3)
        self.go(5, self.rows(2), self.me.at(other_core=True))

    def own_chip(self):
        self.got(2)

    def near_chips(self):
        self.got(4, 2 * TOK)

    def far_chip(self):
        self.got(5)

    def drain(self):
        for n in range(6):
            self.link.sent(self.s + n, self.acts.at[0 : 2 * TOK if n == 4 else TOK])


def eye_mask():
    return lax.broadcasted_iota(jnp.int32, (128, 128), 0) == lax.broadcasted_iota(
        jnp.int32, (128, 128), 1
    )


def kernel(
    length_ref,
    time_ref,
    q_gain_ref,
    k_gain_ref,
    states_hbm,
    mod_hbm,
    wq_hbm,
    wk_hbm,
    wv_hbm,
    wo_hbm,
    next_hbm,
    update_hbm,
    states,
    mod,
    acts,
    w_a,
    w_b,
    w_c,
    w_d,
    w_e,
    o_full,
    raw,
    qk,
    value,
    probs,
    attended,
    squares,
    partial,
    summed,
    z_first,
    z_second,
    pair_out,
    pair_in,
    chain_out,
    chain_in,
    back_out,
    back_in,
    send_sem,
    recv_sem,
    local_sem,
):
    me = Place()
    link = Link(send_sem, recv_sem, me.at(dx=1))

    barrier = pltpu.get_barrier_semaphore()
    for d in range(1, 8):
        pl.semaphore_signal(
            barrier,
            inc=1,
            device_id=(me.step, (me.head + d) % 8, me.x_hi),
            device_id_type=MESH,
        )
    for to in [me.at(dx=1), me.at(dx=-1)] + [me.at(dy=d) for d in (1, 2, 3)]:
        pl.semaphore_signal(barrier, inc=1, device_id=to, device_id_type=MESH)

    y, c = me.y, me.column(0)
    local = []
    for src, dst in (
        (states_hbm.at[0, 0], states),
        (mod_hbm, mod),
        (wq_hbm.at[:, :, 0:256], w_a.at[y, c]),
        (wq_hbm.at[:, :, 256:384], w_b.at[y, c, :, :, 0:128]),
        (wk_hbm.at[:, :, 0:128], w_b.at[y, c, :, :, 128:256]),
        (wk_hbm.at[:, :, 128:384], w_c.at[y, c]),
        (wv_hbm.at[:, :, 0:256], w_d.at[y, c]),
        (wv_hbm.at[:, :, 256:384], w_e.at[y, c]),
        (wo_hbm, o_full.at[:, y, c]),
    ):
        copy = pltpu.make_async_copy(src, dst, local_sem.at[len(local)])
        copy.start()
        local.append(copy)

    def weight(full):
        return PlaneGather(link, me, lambda y, c, h, r: full.at[y, c, h, r], 160)

    def out_weight(first, last):
        return PlaneGather(link, me, lambda y, c, h, r: o_full.at[first:last, y, c, h, r], 32)

    g_a, g_b, g_c, g_d, g_e = (weight(w) for w in (w_a, w_b, w_c, w_d, w_e))
    o_a, o_b, o_c = out_weight(0, 1), out_weight(1, 2), out_weight(2, 5)
    tokens = TokenGather(link, me, acts)

    def product(rows, w):
        return jnp.dot(acts[rows, :], w[...].reshape(5120, w.shape[-1]), preferred_element_type=F32)

    def raw_product(dz, w, column):
        rows = pl.ds(pl.multiple_of(((me.z + dz) % 4) * 256, 256), 256)
        raw[rows, column * 256 : column * 256 + 256] = product(rows, w)

    with jax.named_scope("norm"):
        local[0].wait()
        local[1].wait()
        shift, scale = mod[0], 1.0 + mod[1]

        @pl.loop(0, 4)
        def _(r):
            x = states[pl.ds(pl.multiple_of(r * 32, 32), 32), :]
            centred = x - jnp.mean(x, axis=-1, keepdims=True)
            spread = jnp.mean(centred * centred, axis=-1, keepdims=True)
            out = centred * lax.rsqrt(spread + 1e-06) * scale + shift
            acts[pl.ds(pl.multiple_of(me.head * TOK + r * 32, 32), 32), :] = out.astype(BF16)

    with jax.named_scope("barrier"):
        local[2].wait()
        pl.semaphore_wait(barrier, 12)
    with jax.named_scope("a1"):
        g_a.start1()
        tokens.start1()
        for copy in local[3:]:
            copy.wait()
        g_b.start1()
    with jax.named_scope("a2"):
        g_a.start2()
        g_c.start1()
    with jax.named_scope("b2"):
        g_b.start2()
    with jax.named_scope("a3"):
        g_a.start3()
    with jax.named_scope("a4"):
        g_a.start4()
        g_c.start2()
        g_b.start3()
        g_d.start1()
    with jax.named_scope("tokens2"):
        tokens.start2()
    with jax.named_scope("a5"):
        g_a.finish()
        tokens.own_chip()
    with jax.named_scope("own_a"):
        raw_product(0, w_a, 0)
    with jax.named_scope("b4"):
        g_b.start4()
        g_d.start2()
        g_c.start3()
        g_e.start1()
    with jax.named_scope("tokens3"):
        tokens.start3()
    with jax.named_scope("b5"):
        g_b.finish()
    with jax.named_scope("own_b"):
        raw_product(0, w_b, 1)
    with jax.named_scope("near_wait"):
        tokens.near_chips()
    with jax.named_scope("near_ab"):

        @pl.loop(0, 2)
        def _(i):
            raw_product(2 * i + 3, w_a, 0)
            raw_product(2 * i + 3, w_b, 1)

    with jax.named_scope("c4"):
        g_c.start4()
        g_e.start2()
        g_d.start3()
        o_a.start1()
    with jax.named_scope("tokens4"):
        tokens.start4()
    with jax.named_scope("c5"):
        g_c.finish()
    with jax.named_scope("near_c"):

        @pl.loop(0, 3)
        def _(i):
            raw_product(i + 3, w_c, 2)

    with jax.named_scope("far_wait"):
        tokens.far_chip()
    with jax.named_scope("far"):
        raw_product(2, w_a, 0)
        raw_product(2, w_b, 1)
        raw_product(2, w_c, 2)
    with jax.named_scope("squares"):

        @pl.loop(0, 8)
        def _(b):
            rows = pl.ds(pl.multiple_of(b * 128, 128), 128)
            for part in range(2):
                p = raw[rows, part * LOCAL : (part + 1) * LOCAL]
                total = jnp.sum(p * p, axis=1, keepdims=True)
                row = jnp.sum(jnp.where(eye_mask(), total, 0.0), axis=0, keepdims=True)
                squares[me.head, pl.ds(part * 8 + b, 1), :] = row

        s_squares, r_squares = link.take(1, 1)
        for d in range(1, 8):
            own = squares.at[me.head]
            to = (me.step, (me.head + d) % 8, me.x_hi)
            link.copy(own, own, s_squares, r_squares, to).start()
    length = length_ref[0]

    def softmax(h, m):
        rows = pl.ds(pl.multiple_of(m * 256, 256), 256)
        valid = lax.broadcasted_iota(jnp.int32, (256, 1024), 1) < length
        q = qk[rows, h * HD : (h + 1) * HD]
        k = qk[:, LOCAL + h * HD : LOCAL + (h + 1) * HD]
        s = lax.dot_general(q, k, (((1,), (1,)), ((), ())), preferred_element_type=F32)
        s = jnp.where(valid, s * (math.log2(math.e) / math.sqrt(HD)), -jnp.inf)
        e = jnp.exp2(s - jnp.max(s, axis=-1, keepdims=True))
        probs[h, rows, :] = (e * (1.0 / jnp.sum(e, axis=-1, keepdims=True))).astype(BF16)

    def attend(h, m):
        rows = pl.ds(pl.multiple_of(m * 256, 256), 256)
        o = jnp.dot(probs[h, rows, :], value[:, h * HD : (h + 1) * HD], preferred_element_type=F32)
        attended[rows, h * HD : (h + 1) * HD] = o.astype(BF16)

    def value_product(w, cols, m):
        rows = pl.ds(pl.multiple_of(m * 256, 256), 256)
        value[rows, cols] = product(rows, w).astype(BF16)

    with jax.named_scope("d4"):
        g_d.start4()
        o_a.start2()
        g_e.start3()
        o_b.start1()
        o_c.start1()
    with jax.named_scope("squares_wait"):
        link.got(r_squares, squares.at[0:7])
        link.sent(s_squares, squares.at[0:7])

    with jax.named_scope("qk_norm"):

        @pl.loop(0, 8)
        def _(b):
            rows = pl.ds(pl.multiple_of(b * 128, 128), 128)
            for part, gain in enumerate((q_gain_ref, k_gain_ref)):
                total = squares[0, pl.ds(part * 8 + b, 1), :]
                for d in range(1, 8):
                    total = total + squares[d, pl.ds(part * 8 + b, 1), :]
                factor = lax.rsqrt(total / 3072.0 + 1e-06)
                column = jnp.sum(jnp.where(eye_mask(), factor, 0.0), axis=1, keepdims=True)
                cols = slice(part * LOCAL, (part + 1) * LOCAL)
                qk[rows, cols] = (raw[rows, cols] * column * gain[...].reshape(1, LOCAL)).astype(BF16)

    with jax.named_scope("softmax0"):

        @pl.loop(0, 4)
        def _(m):
            softmax(0, m)

    with jax.named_scope("o_a3"):
        o_a.start3()
    with jax.named_scope("softmax1"):

        @pl.loop(0, 4)
        def _(m):
            softmax(1, m)

    with jax.named_scope("d5"):
        g_d.finish()
    with jax.named_scope("e4"):
        g_e.start4()
        o_b.start2()
        o_c.start2()
    with jax.named_scope("value_d"):

        @pl.loop(0, 4)
        def _(m):
            value_product(w_d, slice(0, 256), m)

    with jax.named_scope("o_b3"):
        o_a.start4()
        o_b.start3()
    with jax.named_scope("softmax2"):

        @pl.loop(0, 4)
        def _(m):
            softmax(2, m)

    with jax.named_scope("attend01"):

        @pl.loop(0, 4)
        def _(m):
            attend(0, m)
            attend(1, m)

    with jax.named_scope("e5"):
        g_e.finish()
        o_c.start3()
    with jax.named_scope("value_e"):

        @pl.loop(0, 4)
        def _(m):
            value_product(w_e, slice(256, 384), m)

    with jax.named_scope("o_b4"):
        o_b.start4()
    with jax.named_scope("attend2"):

        @pl.loop(0, 4)
        def _(m):
            attend(2, m)

    with jax.named_scope("o_a5"):
        o_a.finish()
        for g in (g_a, g_b, g_c, g_d, g_e, tokens):
            g.drain()

    kinds = [link.take(FLIGHT, NJ if kind == 4 else AHEAD) for kind in range(6)]
    sib, first, second, pair, chain, back = range(6)
    up, down = me.at(dz=1), me.at(dz=-1)
    above, below, far = (me.z + 1) % 4, (me.z - 1) % 4, (me.z + 2) % 4
    partner = (me.y * 2 + 1 - me.x_lo, me.head, me.x_hi)
    later = [me.at(dy=d) for d in (1, 2, 3)]
    on_low = me.x_lo == 0
    lower = lax.broadcasted_iota(jnp.int32, (TOK, 128), 1) < 64
    width = (jnp.full((1, 128), time_ref[0, 1] - time_ref[0, 0], jnp.int32)).astype(F32) / 1000.0

    def send_of(kind, j):
        return kinds[kind][0] + j % FLIGHT

    def recv_of(kind, j):
        return kinds[kind][1] + (j if kind == chain else j % AHEAD)

    def go(kind, j, src, dst, to):
        link.copy(src, dst, send_of(kind, j), recv_of(kind, j), to).start()

    def got(kind, j, size):
        link.got(recv_of(kind, j), size)

    def sent(kind, j, size):
        link.sent(send_of(kind, j), size)

    def quarter(n):
        return pl.ds(pl.multiple_of(n * 1280, 128), 1280)

    def next_out(n):
        return pltpu.make_async_copy(states.at[:, quarter(n)], next_hbm.at[:, quarter(n)], local_sem.at[n])

    def update_out(n):
        return pltpu.make_async_copy(
            acts.at[0:TOK, quarter(n)], update_hbm.at[:, quarter(n)], local_sem.at[4 + n]
        )

    def natural(j, m):
        piece, tile = j // 4, (j % 4) * 2 + m
        odd = piece % 2
        low = 5 * tile + (piece + 5 * odd) // 2
        high = 5 * tile + 2 * (1 - odd) + (piece - odd) // 2
        return (
            pl.ds(pl.multiple_of(low * 128, 128), 128),
            pl.ds(pl.multiple_of(high * 128, 128), 128),
        )

    def kept(j, half):
        start = (j % 8) * 128 + half * 64
        return pl.ds(pl.multiple_of(start, 64), 64), pl.ds(pl.multiple_of((j // 8) * 256, 256), 256)

    def project(j):
        w = o_full[j // 4, j % 4].reshape(CW, LOCAL)
        for m in range(4):
            p = lax.dot_general(
                attended[m * 256 : (m + 1) * 256, :],
                w,
                (((1,), (1,)), ((), ())),
                preferred_element_type=F32,
            ).astype(BF16)
            partial[j % SLOTS, m, 0] = p[0:128]
            partial[j % SLOTS, m, 1] = p[128:256]
        go(sib, j, partial.at[j % SLOTS, :, 1 - me.core], summed.at[j], me.at(other_core=True))

    def add_sibling(j):
        got(sib, j, summed.at[j])
        for m in range(4):
            own = partial[j % SLOTS, m, me.core].astype(F32)
            summed[j, m] = (own + summed[j, m].astype(F32)).astype(BF16)
        sent(sib, j, summed.at[j])
        go(first, j, summed.at[j, far, 0:64], z_first.at[j, 0], up)
        go(first, j, summed.at[j, far, 64:128], z_first.at[j, 1], down)

    def add_far(j):
        got(first, j, z_first.at[j])
        summed[j, above, 0:64] = (
            summed[j, above, 0:64].astype(F32) + z_first[j, 0].astype(F32)
        ).astype(BF16)
        summed[j, below, 64:128] = (
            summed[j, below, 64:128].astype(F32) + z_first[j, 1].astype(F32)
        ).astype(BF16)
        go(second, j, summed.at[j, above], z_second.at[j, 0], up)
        go(second, j, summed.at[j, below], z_second.at[j, 1], down)
        sent(first, j, z_first.at[j])

    def drift(j):
        got(second, j, z_second.at[j])
        rows = pl.ds(pl.multiple_of((j % 8) * 128, 128), 128)
        for m in range(2):
            lanes = slice(m * 128, (m + 1) * 128)
            total = (
                summed[j, me.z, :, lanes].astype(F32)
                + z_second[j, 0, :, lanes].astype(F32)
                + z_second[j, 1, :, lanes].astype(F32)
            )
            projected = jnp.where((j // 4) % 2 == 1, pltpu.roll(total, 64, 1), total)
            low, high = natural(j, m)
            gate = jnp.where(lower[0:1], mod[2, :, low], mod[2, :, high])
            branch = gate * projected
            acts[0:TOK, low] = jnp.where(lower, branch, acts[0:TOK, low].astype(F32)).astype(BF16)
            acts[0:TOK, high] = jnp.where(lower, acts[0:TOK, high].astype(F32), branch).astype(BF16)
            current = jnp.where(lower, states[:, low], states[:, high])
            anchor = jnp.where(me.step == 0, current, 0.0)
            raw[rows, pl.ds(pl.multiple_of((j // 8) * 256 + m * 128, 128), 128)] = (
                width * (current + branch) + anchor
            )
        pair_out[j] = raw[kept(j, 1 - me.x_lo)].astype(BF16)
        go(pair, j, pair_out.at[j], pair_in.at[j], partner)

        @pl.when(j >= NJ - 4)
        def _():
            update_out(j % 4).start()

        sent(second, j, z_second.at[j])

    def add_pair(j):
        got(pair, j, pair_in.at[j])
        chain_out[j] = (raw[kept(j, me.x_lo)] + pair_in[j].astype(F32)).astype(BF16)
        for d in (1, 2, 3):

            @pl.when(me.y + d < 4)
            def _(d=d):
                go(chain, j, chain_out.at[j], chain_in.at[j, d - 1], later[d - 1])

        sent(pair, j, pair_in.at[j])

    def add_earlier(j):
        for d in (1, 2, 3):

            @pl.when(me.y == d)
            def _(d=d):
                got(chain, j, chain_in.at[j, 0:d])

        earlier = jnp.zeros((64, CW), F32)
        for d in (1, 2, 3):
            earlier = earlier + jnp.where(me.y >= d, chain_in[j, d - 1].astype(F32), 0.0)
        mine = kept(j, me.x_lo)
        own = raw[mine]
        back_out[j] = (earlier + jnp.where(on_low, own, 0.0)).astype(BF16)
        go(back, j, back_out.at[j], back_in.at[j], partner)
        raw[mine] = own + (earlier + jnp.where(on_low, 0.0, pair_in[j].astype(F32)))
        for d in (1, 2, 3):

            @pl.when(me.y + d == 3)
            def _(d=d):
                sent(chain, j, chain_in.at[j, 0:d])

    def add_back(j):
        got(back, j, back_in.at[j])
        other = kept(j, 1 - me.x_lo)
        raw[other] = raw[other] + back_in[j].astype(F32)
        rows = pl.ds(pl.multiple_of((j % 8) * 128, 128), 128)
        for m in range(2):
            low, high = natural(j, m)
            total = raw[rows, pl.ds(pl.multiple_of((j // 8) * 256 + m * 128, 128), 128)]
            states[:, low] = jnp.where(lower, total, states[:, low])
            states[:, high] = jnp.where(lower, states[:, high], total)

        @pl.when(j >= NJ - 4)
        def _():
            next_out(j % 4).start()

        sent(back, j, back_in.at[j])

    with jax.named_scope("reduce"):
        stages = (project, add_sibling, add_far, drift, add_pair, add_earlier, add_back)

        @pl.loop(0, NJ + LAGS[-1])
        def _(i):
            @pl.when(i == 4)
            def _():
                o_b.finish()

            @pl.when(i == 3)
            def _():
                o_c.start4()

            @pl.when(i == 8)
            def _():
                o_c.finish()

            for lag, stage in zip(LAGS, stages):
                j = i - lag

                @pl.when((j >= 0) & (j < NJ))
                def _(stage=stage, j=j):
                    stage(j)

    with jax.named_scope("drain"):
        for g in (o_a, o_b, o_c):
            g.drain()
    with jax.named_scope("results"):
        for n in range(4):
            update_out(n).wait()
            next_out(n).wait()


def body(states, timesteps, lengths, modulation, w_query, w_key, w_value, w_out, q_gain, k_gain):
    n_send = 8 * 4 + 6 + 1 + 6 * FLIGHT
    n_recv = 8 * 6 + 6 + 1 + 5 * AHEAD + NJ
    vmem = pl.BlockSpec(memory_space=pltpu.VMEM)
    smem = pl.BlockSpec(memory_space=pltpu.SMEM)
    anywhere = pl.BlockSpec(memory_space=pl.ANY)
    nxt, update = pl.pallas_call(
        kernel,
        out_shape=(
            jax.ShapeDtypeStruct((TOK, 5120), F32),
            jax.ShapeDtypeStruct((TOK, 5120), BF16),
        ),
        in_specs=[smem, smem, vmem, vmem] + [anywhere] * 6,
        out_specs=(anywhere, anywhere),
        scratch_shapes=[
            pltpu.VMEM((TOK, 5120), F32),
            pltpu.VMEM((3, 1, 5120), F32),
            pltpu.VMEM((1024, 5120), BF16),
            pltpu.VMEM((4, 4, 2, 160, 256), BF16),
            pltpu.VMEM((4, 4, 2, 160, 256), BF16),
            pltpu.VMEM((4, 4, 2, 160, 256), BF16),
            pltpu.VMEM((4, 4, 2, 160, 256), BF16),
            pltpu.VMEM((4, 4, 2, 160, 128), BF16),
            pltpu.VMEM((PIECES, 4, 4, 2, 32, LOCAL), BF16),
            pltpu.VMEM((1024, 2 * LOCAL), F32),
            pltpu.VMEM((1024, 2 * LOCAL), BF16),
            pltpu.VMEM((1024, LOCAL), BF16),
            pltpu.VMEM((3, 1024, 1024), BF16),
            pltpu.VMEM((1024, LOCAL), BF16),
            pltpu.VMEM((8, 16, 128), F32),
            pltpu.VMEM((SLOTS, 4, 2, TOK, CW), BF16),
            pltpu.VMEM((NJ, 4, TOK, CW), BF16),
            pltpu.VMEM((NJ, 2, 64, CW), BF16),
            pltpu.VMEM((NJ, 2, TOK, CW), BF16),
            pltpu.VMEM((NJ, 64, CW), BF16),
            pltpu.VMEM((NJ, 64, CW), BF16),
            pltpu.VMEM((NJ, 64, CW), BF16),
            pltpu.VMEM((NJ, 3, 64, CW), BF16),
            pltpu.VMEM((NJ, 64, CW), BF16),
            pltpu.VMEM((NJ, 64, CW), BF16),
            pltpu.SemaphoreType.DMA((n_send,)),
            pltpu.SemaphoreType.DMA((n_recv,)),
            pltpu.SemaphoreType.DMA((9,)),
        ],
        compiler_params=pltpu.CompilerParams(
            collective_id=0,
            has_side_effects=True,
            vmem_limit_bytes=63 * 1024 * 1024,
        ),
    )(
        lengths,
        timesteps,
        q_gain,
        k_gain,
        states,
        modulation.transpose(1, 0, 2),
        w_query.reshape(2, 160, LOCAL),
        w_key.reshape(2, 160, LOCAL),
        w_value.reshape(2, 160, LOCAL),
        w_out.T.reshape(PIECES, 2, 32, LOCAL),
    )
    return (nxt[None, None], update[None, None])


def solution(mesh):
    in_specs = (
        P("step", "fsdp", "head", None),
        P("step", None),
        P("fsdp"),
        P("step", None, None),
        P(("step", "fsdp"), "head"),
        P(("step", "fsdp"), "head"),
        P(("step", "fsdp"), "head"),
        P("head", ("step", "fsdp")),
        P("head"),
        P("head"),
    )
    out_specs = (P("step", "fsdp", "head", None), P("step", "fsdp", "head", None))
    return jax.shard_map(body, mesh=mesh, in_specs=in_specs, out_specs=out_specs, check_vma=False)
```

```python
import math

import jax
import jax.numpy as jnp
from jax import lax
from jax.experimental import pallas as pl
from jax.experimental.pallas import tpu as pltpu
from jax.sharding import PartitionSpec as P

HD = 128
BF16 = jnp.bfloat16
F32 = jnp.float32
MESH = pl.DeviceIdType.MESH
TOK = 128
LOCAL = 384
PIECES = 5
NJ = 20
CW = 256
LAGS = (0, 1, 3, 5, 7, 9, 11)
SLOTS = 2
FLIGHT = 4
AHEAD = 8


class Link:
    def __init__(self, send, recv, some_device):
        self.send, self.recv, self.to = send, recv, some_device
        self.sends, self.recvs = 0, 0

    def take(self, sends, recvs):
        first = self.sends, self.recvs
        self.sends, self.recvs = self.sends + sends, self.recvs + recvs
        return first

    def copy(self, src, dst, send, recv, to):
        return pltpu.make_async_remote_copy(
            src_ref=src,
            dst_ref=dst,
            send_sem=self.send.at[send],
            recv_sem=self.recv.at[recv],
            device_id=to,
            device_id_type=MESH,
        )

    def sent(self, send, size):
        self.copy(size, size, send, 0, self.to).wait_send()

    def got(self, recv, size):
        self.copy(size, size, 0, recv, self.to).wait_recv()


class Place:
    def __init__(self):
        step, head, fsdp = (lax.axis_index(a) for a in ("step", "head", "fsdp"))
        self.step, self.head = step, head
        self.y, self.x_lo, self.x_hi = step // 2, step % 2, fsdp
        self.x = self.x_hi * 2 + self.x_lo
        self.z, self.core = head // 2, head % 2

    def at(self, dx=0, dy=0, dz=0, other_core=False):
        x, y, z = (self.x + dx) % 4, (self.y + dy) % 4, (self.z + dz) % 4
        core = 1 - self.core if other_core else self.core
        return (y * 2 + x % 2, z * 2 + core, x // 2)

    def column(self, dx):
        x = (self.x + dx) % 4
        return (x % 2) * 2 + x // 2

    def row(self, dy):
        return (self.y + dy) % 4


class PlaneGather:
    def __init__(self, link, place, view, half):
        me = place
        whole, low, high = slice(0, half), slice(0, half // 2), slice(half // 2, half)
        every = slice(0, 4)
        y, c = me.y, me.column(0)
        left, right, far_x = me.column(-1), me.column(1), me.column(2)
        below, above, far_y = me.row(-1), me.row(1), me.row(2)
        east, west, north, south = me.at(dx=1), me.at(dx=-1), me.at(dy=1), me.at(dy=-1)
        self.link, self.view = link, view
        self.s, self.r = link.take(4, 6)
        self.sends = (
            ((y, c, 0, whole), east),
            ((y, c, 0, whole), west),
            ((y, c, 1, whole), north),
            ((y, c, 1, whole), south),
            ((y, left, 0, low), east),
            ((y, right, 0, high), west),
            ((below, c, 1, low), north),
            ((above, c, 1, high), south),
            ((y, every, 0, whole), north),
            ((y, every, 0, whole), south),
            ((every, c, 1, whole), east),
            ((every, c, 1, whole), west),
            ((below, every, 0, low), north),
            ((above, every, 0, high), south),
            ((every, left, 1, low), east),
            ((every, right, 1, high), west),
        )
        two = slice(0, 2)
        self.pair = view(y, two, 0, whole)
        self.rows = view(two, every, 0, whole)
        self.half = view(every, every, 0, whole)
        self.row = view(y, every, 0, whole)

    def start(self, first, last):
        for slot in range(first, last):
            args, to = self.sends[slot]
            part = self.view(*args)
            recv = (0, 0, 1, 1, 2, 2, 2, 2, 3, 3, 4, 4, 5, 5, 5, 5)[slot]
            self.link.copy(part, part, self.s + slot // 4, self.r + recv, to).start()

    def got(self, n, size):
        self.link.got(self.r + n, size)

    def start1(self):
        self.start(0, 4)

    def start2(self):
        self.got(0, self.pair)
        self.start(4, 6)
        self.got(1, self.pair)
        self.start(6, 8)

    def start3(self):
        self.got(2, self.pair)
        self.start(8, 12)

    def start4(self):
        self.got(3, self.rows)
        self.start(12, 14)
        self.got(4, self.rows)
        self.start(14, 16)

    def finish(self):
        self.got(5, self.rows)

    def drain(self):
        for phase, size in enumerate((self.row, self.pair, self.half, self.rows)):
            self.link.sent(self.s + phase, size)


class TokenGather:
    def __init__(self, link, place, acts):
        self.link, self.me, self.acts = link, place, acts
        self.s, self.r = link.take(6, 6)

    def rows(self, dz, start=0, size=TOK):
        me = self.me
        z = (me.z + dz) % 4
        return self.acts.at[pl.ds(pl.multiple_of((z * 2 + me.core) * TOK + start, 64), size), :]

    def low(self, dz):
        return self.rows(dz, 0, 64)

    def high(self, dz):
        return self.rows(dz, 64, 64)

    def go(self, n, part, to):
        self.link.copy(part, part, self.s + n, self.r + n, to).start()

    def got(self, n, rows=TOK):
        self.link.got(self.r + n, self.acts.at[0:rows])

    def start1(self):
        up, down = self.me.at(dz=1), self.me.at(dz=-1)
        self.go(0, self.low(0), up)
        self.go(0, self.high(0), down)
        self.go(1, self.high(0), up)
        self.go(1, self.low(0), down)
        self.go(2, self.rows(0), self.me.at(other_core=True))

    def start2(self):
        self.got(0)
        self.go(3, self.low(-1), self.me.at(dz=1))
        self.go(3, self.high(1), self.me.at(dz=-1))

    def start3(self):
        other = self.me.at(other_core=True)
        self.got(1)
        self.go(4, self.rows(-1), other)
        self.go(4, self.rows(1), other)

    def start4(self):
        self.got(3)
        self.go(5, self.rows(2), self.me.at(other_core=True))

    def own_chip(self):
        self.got(2)

    def near_chips(self):
        self.got(4, 2 * TOK)

    def far_chip(self):
        self.got(5)

    def drain(self):
        for n in range(6):
            self.link.sent(self.s + n, self.acts.at[0 : 2 * TOK if n == 4 else TOK])


def eye_mask():
    return lax.broadcasted_iota(jnp.int32, (128, 128), 0) == lax.broadcasted_iota(
        jnp.int32, (128, 128), 1
    )


def kernel(
    length_ref,
    time_ref,
    q_gain_ref,
    k_gain_ref,
    states_hbm,
    mod_hbm,
    wq_hbm,
    wk_hbm,
    wv_hbm,
    wo_hbm,
    next_ref,
    update_ref,
    states,
    mod,
    acts,
    w_a,
    w_b,
    w_c,
    w_d,
    w_e,
    o_full,
    raw,
    qk,
    value,
    probs,
    attended,
    squares,
    partial,
    summed,
    z_first,
    z_second,
    pair_out,
    pair_in,
    chain_out,
    chain_in,
    back_out,
    back_in,
    send_sem,
    recv_sem,
    local_sem,
):
    me = Place()
    link = Link(send_sem, recv_sem, me.at(dx=1))

    barrier = pltpu.get_barrier_semaphore()
    for d in range(1, 8):
        pl.semaphore_signal(
            barrier,
            inc=1,
            device_id=(me.step, (me.head + d) % 8, me.x_hi),
            device_id_type=MESH,
        )
    for to in [me.at(dx=1), me.at(dx=-1)] + [me.at(dy=d) for d in (1, 2, 3)]:
        pl.semaphore_signal(barrier, inc=1, device_id=to, device_id_type=MESH)

    y, c = me.y, me.column(0)
    local = []
    for src, dst in (
        (states_hbm.at[0, 0], states),
        (mod_hbm, mod),
        (wq_hbm.at[:, :, 0:256], w_a.at[y, c]),
        (wq_hbm.at[:, :, 256:384], w_b.at[y, c, :, :, 0:128]),
        (wk_hbm.at[:, :, 0:128], w_b.at[y, c, :, :, 128:256]),
        (wk_hbm.at[:, :, 128:384], w_c.at[y, c]),
        (wv_hbm.at[:, :, 0:256], w_d.at[y, c]),
        (wv_hbm.at[:, :, 256:384], w_e.at[y, c]),
        (wo_hbm, o_full.at[:, y, c]),
    ):
        copy = pltpu.make_async_copy(src, dst, local_sem.at[len(local)])
        copy.start()
        local.append(copy)

    def weight(full):
        return PlaneGather(link, me, lambda y, c, h, r: full.at[y, c, h, r], 160)

    def out_weight(first, last):
        return PlaneGather(link, me, lambda y, c, h, r: o_full.at[first:last, y, c, h, r], 32)

    g_a, g_b, g_c, g_d, g_e = (weight(w) for w in (w_a, w_b, w_c, w_d, w_e))
    o_a, o_b, o_c = out_weight(0, 1), out_weight(1, 2), out_weight(2, 5)
    tokens = TokenGather(link, me, acts)

    def product(rows, w):
        return jnp.dot(acts[rows, :], w[...].reshape(5120, w.shape[-1]), preferred_element_type=F32)

    def raw_product(dz, w, column):
        rows = pl.ds(pl.multiple_of(((me.z + dz) % 4) * 256, 256), 256)
        raw[rows, column * 256 : column * 256 + 256] = product(rows, w)

    with jax.named_scope("norm"):
        local[0].wait()
        local[1].wait()
        shift, scale = mod[0], 1.0 + mod[1]

        @pl.loop(0, 4)
        def _(r):
            x = states[pl.ds(pl.multiple_of(r * 32, 32), 32), :]
            centred = x - jnp.mean(x, axis=-1, keepdims=True)
            spread = jnp.mean(centred * centred, axis=-1, keepdims=True)
            out = centred * lax.rsqrt(spread + 1e-06) * scale + shift
            acts[pl.ds(pl.multiple_of(me.head * TOK + r * 32, 32), 32), :] = out.astype(BF16)

        for h in range(3):
            value[h, :, HD : 2 * HD] = jnp.ones((1024, HD), BF16)

    with jax.named_scope("barrier"):
        local[2].wait()
        pl.semaphore_wait(barrier, 12)
    with jax.named_scope("a1"):
        g_a.start1()
        tokens.start1()
        for copy in local[3:]:
            copy.wait()
        g_b.start1()
    with jax.named_scope("a2"):
        g_a.start2()
        g_c.start1()
    with jax.named_scope("b2"):
        g_b.start2()
    with jax.named_scope("a3"):
        g_a.start3()
    with jax.named_scope("a4"):
        g_a.start4()
        g_c.start2()
        g_b.start3()
        g_d.start1()
    with jax.named_scope("tokens2"):
        tokens.start2()
    with jax.named_scope("a5"):
        g_a.finish()
        tokens.own_chip()
    with jax.named_scope("own_a"):
        raw_product(0, w_a, 0)
    with jax.named_scope("b4"):
        g_b.start4()
        g_d.start2()
        g_c.start3()
        g_e.start1()
    with jax.named_scope("tokens3"):
        tokens.start3()
    with jax.named_scope("b5"):
        g_b.finish()
    with jax.named_scope("own_b"):
        raw_product(0, w_b, 1)
    with jax.named_scope("near_wait"):
        tokens.near_chips()
    with jax.named_scope("near_ab"):

        @pl.loop(0, 2)
        def _(i):
            raw_product(2 * i + 3, w_a, 0)
            raw_product(2 * i + 3, w_b, 1)

    with jax.named_scope("c4"):
        g_c.start4()
        g_e.start2()
        g_d.start3()
        o_a.start1()
    with jax.named_scope("tokens4"):
        tokens.start4()
    with jax.named_scope("far_wait"):
        tokens.far_chip()
    with jax.named_scope("far_ab"):
        raw_product(2, w_a, 0)
        raw_product(2, w_b, 1)
    with jax.named_scope("c5"):
        g_c.finish()
        g_e.start3()
    with jax.named_scope("all_c"):

        @pl.loop(0, 4)
        def _(i):
            raw_product(i, w_c, 2)

    with jax.named_scope("squares"):

        @pl.loop(0, 8)
        def _(b):
            rows = pl.ds(pl.multiple_of(b * 128, 128), 128)
            for part in range(2):
                p = raw[rows, part * LOCAL : (part + 1) * LOCAL]
                total = jnp.sum(p * p, axis=1, keepdims=True)
                row = jnp.sum(jnp.where(eye_mask(), total, 0.0), axis=0, keepdims=True)
                squares[me.head, pl.ds(part * 8 + b, 1), :] = row

        s_squares, r_squares = link.take(1, 1)
        for d in range(1, 8):
            own = squares.at[me.head]
            to = (me.step, (me.head + d) % 8, me.x_hi)
            link.copy(own, own, s_squares, r_squares, to).start()
    length = length_ref[0]

    def softmax(h, m):
        rows = pl.ds(pl.multiple_of(m * 256, 256), 256)
        valid = lax.broadcasted_iota(jnp.int32, (256, 512), 1) < length - 512
        q = qk[rows, h * HD : (h + 1) * HD]
        k = qk[:, LOCAL + h * HD : LOCAL + (h + 1) * HD]
        s = lax.dot_general(q, k, (((1,), (1,)), ((), ())), preferred_element_type=F32)
        s = s * (math.log2(math.e) / math.sqrt(HD))
        s = jnp.concatenate([s[:, 0:512], jnp.where(valid, s[:, 512:1024], -jnp.inf)], axis=1)
        probs[h, rows, :] = jnp.exp2(s - jnp.max(s, axis=-1, keepdims=True)).astype(BF16)

    def attend(h, m):
        rows = pl.ds(pl.multiple_of(m * 256, 256), 256)
        o = jnp.dot(probs[h, rows, :], value[h], preferred_element_type=F32)
        attended[rows, h * HD : (h + 1) * HD] = (o[:, 0:HD] / o[:, HD : 2 * HD]).astype(BF16)

    def value_product(w, heads, m):
        rows = pl.ds(pl.multiple_of(m * 256, 256), 256)
        v = product(rows, w).astype(BF16)
        for n, h in enumerate(heads):
            value[h, rows, 0:HD] = v[:, n * HD : (n + 1) * HD]

    with jax.named_scope("d4"):
        g_d.start4()
        o_a.start2()
        o_b.start1()
        g_e.start4()
    with jax.named_scope("squares_wait"):
        link.got(r_squares, squares.at[0:7])
        link.sent(s_squares, squares.at[0:7])

    with jax.named_scope("qk_norm"):

        @pl.loop(0, 8)
        def _(b):
            rows = pl.ds(pl.multiple_of(b * 128, 128), 128)
            for part, gain in enumerate((q_gain_ref, k_gain_ref)):
                total = squares[0, pl.ds(part * 8 + b, 1), :]
                for d in range(1, 8):
                    total = total + squares[d, pl.ds(part * 8 + b, 1), :]
                factor = lax.rsqrt(total / 3072.0 + 1e-06)
                column = jnp.sum(jnp.where(eye_mask(), factor, 0.0), axis=1, keepdims=True)
                cols = slice(part * LOCAL, (part + 1) * LOCAL)
                qk[rows, cols] = (raw[rows, cols] * column * gain[...].reshape(1, LOCAL)).astype(BF16)

    with jax.named_scope("softmax0"):

        @pl.loop(0, 4)
        def _(m):
            softmax(0, m)

    with jax.named_scope("o_a3"):
        o_a.start3()
        o_b.start2()
        o_c.start1()
    with jax.named_scope("d5"):
        g_d.finish()
    with jax.named_scope("softmax1_value_d"):

        @pl.loop(0, 4)
        def _(m):
            softmax(1, m)
            value_product(w_d, (0, 1), m)

    with jax.named_scope("o_b3"):
        o_a.start4()
        o_b.start3()
    with jax.named_scope("e5"):
        g_e.finish()
        o_c.start2()
    with jax.named_scope("softmax2_value_e"):

        @pl.loop(0, 4)
        def _(m):
            softmax(2, m)
            value_product(w_e, (2,), m)

    with jax.named_scope("o_b4"):
        o_b.start4()
        o_c.start3()
    with jax.named_scope("attend"):

        @pl.loop(0, 4)
        def _(m):
            for h in range(3):
                attend(h, m)

    with jax.named_scope("o_a5"):
        o_a.finish()
        for g in (g_a, g_b, g_c, g_d, g_e, tokens):
            g.drain()

    kinds = [link.take(FLIGHT, NJ if kind == 4 else AHEAD) for kind in range(6)]
    sib, first, second, pair, chain, back = range(6)
    up, down = me.at(dz=1), me.at(dz=-1)
    above, below, far = (me.z + 1) % 4, (me.z - 1) % 4, (me.z + 2) % 4
    partner = (me.y * 2 + 1 - me.x_lo, me.head, me.x_hi)
    later = [me.at(dy=d) for d in (1, 2, 3)]
    on_low = me.x_lo == 0
    lower = lax.broadcasted_iota(jnp.int32, (TOK, 128), 1) < 64
    width = (jnp.full((1, 128), time_ref[0, 1] - time_ref[0, 0], jnp.int32)).astype(F32) / 1000.0

    def send_of(kind, j):
        return kinds[kind][0] + j % FLIGHT

    def recv_of(kind, j):
        return kinds[kind][1] + (j if kind == chain else j % AHEAD)

    def go(kind, j, src, dst, to):
        link.copy(src, dst, send_of(kind, j), recv_of(kind, j), to).start()

    def got(kind, j, size):
        link.got(recv_of(kind, j), size)

    def sent(kind, j, size):
        link.sent(send_of(kind, j), size)

    def natural(j, m):
        piece, tile = j // 4, (j % 4) * 2 + m
        odd = piece % 2
        low = 5 * tile + (piece + 5 * odd) // 2
        high = 5 * tile + 2 * (1 - odd) + (piece - odd) // 2
        return (
            pl.ds(pl.multiple_of(low * 128, 128), 128),
            pl.ds(pl.multiple_of(high * 128, 128), 128),
        )

    def kept(j, half):
        start = (j % 8) * 128 + half * 64
        return pl.ds(pl.multiple_of(start, 64), 64), pl.ds(pl.multiple_of((j // 8) * 256, 256), 256)

    def project(j):
        w = o_full[j // 4, j % 4].reshape(CW, LOCAL)
        for m in range(4):
            p = lax.dot_general(
                attended[m * 256 : (m + 1) * 256, :],
                w,
                (((1,), (1,)), ((), ())),
                preferred_element_type=F32,
            ).astype(BF16)
            partial[j % SLOTS, m, 0] = p[0:128]
            partial[j % SLOTS, m, 1] = p[128:256]
        go(sib, j, partial.at[j % SLOTS, :, 1 - me.core], summed.at[j], me.at(other_core=True))

    def add_sibling(j):
        got(sib, j, summed.at[j])
        for m in range(4):
            own = partial[j % SLOTS, m, me.core].astype(F32)
            summed[j, m] = (own + summed[j, m].astype(F32)).astype(BF16)
        sent(sib, j, summed.at[j])
        go(first, j, summed.at[j, far, 0:64], z_first.at[j, 0], up)
        go(first, j, summed.at[j, far, 64:128], z_first.at[j, 1], down)

    def add_far(j):
        got(first, j, z_first.at[j])
        summed[j, above, 0:64] = (
            summed[j, above, 0:64].astype(F32) + z_first[j, 0].astype(F32)
        ).astype(BF16)
        summed[j, below, 64:128] = (
            summed[j, below, 64:128].astype(F32) + z_first[j, 1].astype(F32)
        ).astype(BF16)
        go(second, j, summed.at[j, above], z_second.at[j, 0], up)
        go(second, j, summed.at[j, below], z_second.at[j, 1], down)
        sent(first, j, z_first.at[j])

    def drift(j):
        got(second, j, z_second.at[j])
        rows = pl.ds(pl.multiple_of((j % 8) * 128, 128), 128)
        for m in range(2):
            lanes = slice(m * 128, (m + 1) * 128)
            total = (
                summed[j, me.z, :, lanes].astype(F32)
                + z_second[j, 0, :, lanes].astype(F32)
                + z_second[j, 1, :, lanes].astype(F32)
            )
            projected = jnp.where((j // 4) % 2 == 1, pltpu.roll(total, 64, 1), total)
            low, high = natural(j, m)
            gate = jnp.where(lower[0:1], mod[2, :, low], mod[2, :, high])
            branch = gate * projected
            update_ref[:, low] = jnp.where(lower, branch, update_ref[:, low].astype(F32)).astype(BF16)
            update_ref[:, high] = jnp.where(lower, update_ref[:, high].astype(F32), branch).astype(BF16)
            current = jnp.where(lower, states[:, low], states[:, high])
            anchor = jnp.where(me.step == 0, current, 0.0)
            raw[rows, pl.ds(pl.multiple_of((j // 8) * 256 + m * 128, 128), 128)] = (
                width * (current + branch) + anchor
            )
        pair_out[j] = raw[kept(j, 1 - me.x_lo)].astype(BF16)
        go(pair, j, pair_out.at[j], pair_in.at[j], partner)
        sent(second, j, z_second.at[j])

    def add_pair(j):
        got(pair, j, pair_in.at[j])
        chain_out[j] = (raw[kept(j, me.x_lo)] + pair_in[j].astype(F32)).astype(BF16)
        for d in (1, 2, 3):

            @pl.when(me.y + d < 4)
            def _(d=d):
                go(chain, j, chain_out.at[j], chain_in.at[j, d - 1], later[d - 1])

        sent(pair, j, pair_in.at[j])

    def add_earlier(j):
        for d in (1, 2, 3):

            @pl.when(me.y == d)
            def _(d=d):
                got(chain, j, chain_in.at[j, 0:d])

        earlier = jnp.zeros((64, CW), F32)
        for d in (1, 2, 3):
            earlier = earlier + jnp.where(me.y >= d, chain_in[j, d - 1].astype(F32), 0.0)
        mine = kept(j, me.x_lo)
        own = raw[mine]
        back_out[j] = (earlier + jnp.where(on_low, own, 0.0)).astype(BF16)
        go(back, j, back_out.at[j], back_in.at[j], partner)
        raw[mine] = own + (earlier + jnp.where(on_low, 0.0, pair_in[j].astype(F32)))
        for d in (1, 2, 3):

            @pl.when(me.y + d == 3)
            def _(d=d):
                sent(chain, j, chain_in.at[j, 0:d])

    def add_back(j):
        got(back, j, back_in.at[j])
        other = kept(j, 1 - me.x_lo)
        raw[other] = raw[other] + back_in[j].astype(F32)
        rows = pl.ds(pl.multiple_of((j % 8) * 128, 128), 128)
        for m in range(2):
            low, high = natural(j, m)
            total = raw[rows, pl.ds(pl.multiple_of((j // 8) * 256 + m * 128, 128), 128)]
            next_ref[:, low] = jnp.where(lower, total, next_ref[:, low])
            next_ref[:, high] = jnp.where(lower, next_ref[:, high], total)
        sent(back, j, back_in.at[j])

    with jax.named_scope("reduce"):
        stages = (project, add_sibling, add_far, drift, add_pair, add_earlier, add_back)

        @pl.loop(0, NJ + LAGS[-1])
        def _(i):
            @pl.when(i == 4)
            def _():
                o_b.finish()

            @pl.when(i == 6)
            def _():
                o_c.start4()

            @pl.when(i == 8)
            def _():
                o_c.finish()

            for lag, stage in zip(LAGS, stages):
                j = i - lag

                @pl.when((j >= 0) & (j < NJ))
                def _(stage=stage, j=j):
                    stage(j)

    with jax.named_scope("drain"):
        for g in (o_a, o_b, o_c):
            g.drain()


def body(states, timesteps, lengths, modulation, w_query, w_key, w_value, w_out, q_gain, k_gain):
    n_send = 8 * 4 + 6 + 1 + 6 * FLIGHT
    n_recv = 8 * 6 + 6 + 1 + 5 * AHEAD + NJ
    vmem = pl.BlockSpec(memory_space=pltpu.VMEM)
    smem = pl.BlockSpec(memory_space=pltpu.SMEM)
    anywhere = pl.BlockSpec(memory_space=pl.ANY)
    nxt, update = pl.pallas_call(
        kernel,
        out_shape=(
            pltpu.VMEM((TOK, 5120), F32),
            pltpu.VMEM((TOK, 5120), BF16),
        ),
        in_specs=[smem, smem, vmem, vmem] + [anywhere] * 6,
        out_specs=(vmem, vmem),
        scratch_shapes=[
            pltpu.VMEM((TOK, 5120), F32),
            pltpu.VMEM((3, 1, 5120), F32),
            pltpu.VMEM((1024, 5120), BF16),
            pltpu.VMEM((4, 4, 2, 160, 256), BF16),
            pltpu.VMEM((4, 4, 2, 160, 256), BF16),
            pltpu.VMEM((4, 4, 2, 160, 256), BF16),
            pltpu.VMEM((4, 4, 2, 160, 256), BF16),
            pltpu.VMEM((4, 4, 2, 160, 128), BF16),
            pltpu.VMEM((PIECES, 4, 4, 2, 32, LOCAL), BF16),
            pltpu.VMEM((1024, 2 * LOCAL), F32),
            pltpu.VMEM((1024, 2 * LOCAL), BF16),
            pltpu.VMEM((3, 1024, 2 * HD), BF16),
            pltpu.VMEM((3, 1024, 1024), BF16),
            pltpu.VMEM((1024, LOCAL), BF16),
            pltpu.VMEM((8, 16, 128), F32),
            pltpu.VMEM((SLOTS, 4, 2, TOK, CW), BF16),
            pltpu.VMEM((NJ, 4, TOK, CW), BF16),
            pltpu.VMEM((NJ, 2, 64, CW), BF16),
            pltpu.VMEM((NJ, 2, TOK, CW), BF16),
            pltpu.VMEM((NJ, 64, CW), BF16),
            pltpu.VMEM((NJ, 64, CW), BF16),
            pltpu.VMEM((NJ, 64, CW), BF16),
            pltpu.VMEM((NJ, 3, 64, CW), BF16),
            pltpu.VMEM((NJ, 64, CW), BF16),
            pltpu.VMEM((NJ, 64, CW), BF16),
            pltpu.SemaphoreType.DMA((n_send,)),
            pltpu.SemaphoreType.DMA((n_recv,)),
            pltpu.SemaphoreType.DMA((9,)),
        ],
        compiler_params=pltpu.CompilerParams(
            collective_id=0,
            has_side_effects=True,
            vmem_limit_bytes=57 * 1024 * 1024,
        ),
    )(
        lengths,
        timesteps,
        q_gain,
        k_gain,
        states,
        modulation.transpose(1, 0, 2),
        w_query.reshape(2, 160, LOCAL),
        w_key.reshape(2, 160, LOCAL),
        w_value.reshape(2, 160, LOCAL),
        w_out.T.reshape(PIECES, 2, 32, LOCAL),
    )
    return (nxt[None, None], update[None, None])


def solution(mesh):
    in_specs = (
        P("step", "fsdp", "head", None),
        P("step", None),
        P("fsdp"),
        P("step", None, None),
        P(("step", "fsdp"), "head"),
        P(("step", "fsdp"), "head"),
        P(("step", "fsdp"), "head"),
        P("head", ("step", "fsdp")),
        P("head"),
        P("head"),
    )
    out_specs = (P("step", "fsdp", "head", None), P("step", "fsdp", "head", None))
    return jax.shard_map(body, mesh=mesh, in_specs=in_specs, out_specs=out_specs, check_vma=False)
```

```python
import math

import jax
import jax.numpy as jnp
from jax import lax
from jax.experimental import pallas as pl
from jax.experimental.pallas import tpu as pltpu
from jax.sharding import PartitionSpec as P

HD = 128
BF16 = jnp.bfloat16
F32 = jnp.float32
MESH = pl.DeviceIdType.MESH
TOK = 128
LOCAL = 384
PIECES = 5
NJ = 20
CW = 256
LAGS = (0, 2, 5, 8, 10, 12, 14)
SLOTS = 3
FLIGHT = 4
AHEAD = 8


class Link:
    def __init__(self, send, recv, some_device):
        self.send, self.recv, self.to = send, recv, some_device
        self.sends, self.recvs = 0, 0

    def take(self, sends, recvs):
        first = self.sends, self.recvs
        self.sends, self.recvs = self.sends + sends, self.recvs + recvs
        return first

    def copy(self, src, dst, send, recv, to):
        return pltpu.make_async_remote_copy(
            src_ref=src,
            dst_ref=dst,
            send_sem=self.send.at[send],
            recv_sem=self.recv.at[recv],
            device_id=to,
            device_id_type=MESH,
        )

    def sent(self, send, size):
        self.copy(size, size, send, 0, self.to).wait_send()

    def got(self, recv, size):
        self.copy(size, size, 0, recv, self.to).wait_recv()


class Place:
    def __init__(self):
        step, head, fsdp = (lax.axis_index(a) for a in ("step", "head", "fsdp"))
        self.step, self.head = step, head
        self.y, self.x_lo, self.x_hi = step // 2, step % 2, fsdp
        self.x = self.x_hi * 2 + self.x_lo
        self.z, self.core = head // 2, head % 2

    def at(self, dx=0, dy=0, dz=0, other_core=False):
        x, y, z = (self.x + dx) % 4, (self.y + dy) % 4, (self.z + dz) % 4
        core = 1 - self.core if other_core else self.core
        return (y * 2 + x % 2, z * 2 + core, x // 2)

    def column(self, dx):
        x = (self.x + dx) % 4
        return (x % 2) * 2 + x // 2

    def row(self, dy):
        return (self.y + dy) % 4


class PlaneGather:
    def __init__(self, link, place, view, half):
        me = place
        whole, low, high = slice(0, half), slice(0, half // 2), slice(half // 2, half)
        every = slice(0, 4)
        y, c = me.y, me.column(0)
        left, right, far_x = me.column(-1), me.column(1), me.column(2)
        below, above, far_y = me.row(-1), me.row(1), me.row(2)
        east, west, north, south = me.at(dx=1), me.at(dx=-1), me.at(dy=1), me.at(dy=-1)
        self.link, self.view = link, view
        self.s, self.r = link.take(4, 6)
        self.sends = (
            ((y, c, 0, whole), east),
            ((y, c, 0, whole), west),
            ((y, c, 1, whole), north),
            ((y, c, 1, whole), south),
            ((y, left, 0, low), east),
            ((y, right, 0, high), west),
            ((below, c, 1, low), north),
            ((above, c, 1, high), south),
            ((y, every, 0, whole), north),
            ((y, every, 0, whole), south),
            ((every, c, 1, whole), east),
            ((every, c, 1, whole), west),
            ((below, every, 0, low), north),
            ((above, every, 0, high), south),
            ((every, left, 1, low), east),
            ((every, right, 1, high), west),
        )
        two = slice(0, 2)
        self.pair = view(y, two, 0, whole)
        self.rows = view(two, every, 0, whole)
        self.half = view(every, every, 0, whole)
        self.row = view(y, every, 0, whole)

    def start(self, first, last):
        for slot in range(first, last):
            args, to = self.sends[slot]
            part = self.view(*args)
            recv = (0, 0, 1, 1, 2, 2, 2, 2, 3, 3, 4, 4, 5, 5, 5, 5)[slot]
            self.link.copy(part, part, self.s + slot // 4, self.r + recv, to).start()

    def got(self, n, size):
        self.link.got(self.r + n, size)

    def start1(self):
        self.start(0, 4)

    def start2(self):
        self.got(0, self.pair)
        self.start(4, 6)
        self.got(1, self.pair)
        self.start(6, 8)

    def start3(self):
        self.got(2, self.pair)
        self.start(8, 12)

    def start4(self):
        self.got(3, self.rows)
        self.start(12, 14)
        self.got(4, self.rows)
        self.start(14, 16)

    def finish(self):
        self.got(5, self.rows)

    def drain(self):
        for phase, size in enumerate((self.row, self.pair, self.half, self.rows)):
            self.link.sent(self.s + phase, size)


class TokenGather:
    def __init__(self, link, place, acts):
        self.link, self.me, self.acts = link, place, acts
        self.s, self.r = link.take(6, 6)

    def rows(self, dz, start=0, size=TOK):
        me = self.me
        z = (me.z + dz) % 4
        return self.acts.at[pl.ds(pl.multiple_of((z * 2 + me.core) * TOK + start, 64), size), :]

    def low(self, dz):
        return self.rows(dz, 0, 64)

    def high(self, dz):
        return self.rows(dz, 64, 64)

    def go(self, n, part, to):
        self.link.copy(part, part, self.s + n, self.r + n, to).start()

    def got(self, n, rows=TOK):
        self.link.got(self.r + n, self.acts.at[0:rows])

    def start1(self):
        up, down = self.me.at(dz=1), self.me.at(dz=-1)
        self.go(0, self.low(0), up)
        self.go(0, self.high(0), down)
        self.go(1, self.high(0), up)
        self.go(1, self.low(0), down)
        self.go(2, self.rows(0), self.me.at(other_core=True))

    def start2(self):
        self.got(0)
        self.go(3, self.low(-1), self.me.at(dz=1))
        self.go(3, self.high(1), self.me.at(dz=-1))

    def start3(self):
        other = self.me.at(other_core=True)
        self.got(1)
        self.go(4, self.rows(-1), other)
        self.go(4, self.rows(1), other)

    def start4(self):
        self.got(3)
        self.go(5, self.rows(2), self.me.at(other_core=True))

    def own_chip(self):
        self.got(2)

    def near_chips(self):
        self.got(4, 2 * TOK)

    def far_chip(self):
        self.got(5)

    def drain(self):
        for n in range(6):
            self.link.sent(self.s + n, self.acts.at[0 : 2 * TOK if n == 4 else TOK])


def eye_mask():
    return lax.broadcasted_iota(jnp.int32, (128, 128), 0) == lax.broadcasted_iota(
        jnp.int32, (128, 128), 1
    )


def kernel(
    length_ref,
    time_ref,
    q_gain_ref,
    k_gain_ref,
    states_hbm,
    mod_hbm,
    wq_hbm,
    wk_hbm,
    wv_hbm,
    wo_hbm,
    next_ref,
    update_ref,
    states,
    mod,
    acts,
    w_a,
    w_b,
    w_c,
    w_d,
    w_e,
    o_full,
    raw,
    qk,
    value,
    probs,
    attended,
    squares,
    partial,
    summed,
    z_first,
    z_second,
    pair_out,
    pair_in,
    chain_out,
    chain_in,
    back_out,
    back_in,
    send_sem,
    recv_sem,
    local_sem,
):
    me = Place()
    link = Link(send_sem, recv_sem, me.at(dx=1))

    barrier = pltpu.get_barrier_semaphore()
    for d in range(1, 8):
        pl.semaphore_signal(
            barrier,
            inc=1,
            device_id=(me.step, (me.head + d) % 8, me.x_hi),
            device_id_type=MESH,
        )
    for to in [me.at(dx=1), me.at(dx=-1)] + [me.at(dy=d) for d in (1, 2, 3)]:
        pl.semaphore_signal(barrier, inc=1, device_id=to, device_id_type=MESH)

    y, c = me.y, me.column(0)
    local = []
    for src, dst in (
        (states_hbm.at[0, 0], states),
        (mod_hbm, mod),
        (wq_hbm.at[:, :, 0:256], w_a.at[y, c]),
        (wq_hbm.at[:, :, 256:384], w_b.at[y, c, :, :, 0:128]),
        (wk_hbm.at[:, :, 0:128], w_b.at[y, c, :, :, 128:256]),
        (wk_hbm.at[:, :, 128:384], w_c.at[y, c]),
        (wv_hbm.at[:, :, 0:256], w_d.at[y, c]),
        (wv_hbm.at[:, :, 256:384], w_e.at[y, c]),
        (wo_hbm, o_full.at[:, y, c]),
    ):
        copy = pltpu.make_async_copy(src, dst, local_sem.at[len(local)])
        copy.start()
        local.append(copy)

    def weight(full):
        return PlaneGather(link, me, lambda y, c, h, r: full.at[y, c, h, r], 160)

    def out_weight(first, last):
        return PlaneGather(link, me, lambda y, c, h, r: o_full.at[first:last, y, c, h, r], 32)

    g_a, g_b, g_c, g_d, g_e = (weight(w) for w in (w_a, w_b, w_c, w_d, w_e))
    o_a, o_b, o_c = out_weight(0, 1), out_weight(1, 2), out_weight(2, 5)
    tokens = TokenGather(link, me, acts)

    def product(rows, w):
        return jnp.dot(acts[rows, :], w[...].reshape(5120, w.shape[-1]), preferred_element_type=F32)

    def raw_product(dz, w, column):
        rows = pl.ds(pl.multiple_of(((me.z + dz) % 4) * 256, 256), 256)
        raw[rows, column * 256 : column * 256 + 256] = product(rows, w)

    with jax.named_scope("norm"):
        local[0].wait()
        local[1].wait()
        shift, scale = mod[0], 1.0 + mod[1]

        @pl.loop(0, 4)
        def _(r):
            x = states[pl.ds(pl.multiple_of(r * 32, 32), 32), :]
            centred = x - jnp.mean(x, axis=-1, keepdims=True)
            spread = jnp.mean(centred * centred, axis=-1, keepdims=True)
            out = centred * lax.rsqrt(spread + 1e-06) * scale + shift
            acts[pl.ds(pl.multiple_of(me.head * TOK + r * 32, 32), 32), :] = out.astype(BF16)

        for h in range(3):
            value[h, :, HD : 2 * HD] = jnp.ones((1024, HD), BF16)

    with jax.named_scope("barrier"):
        local[2].wait()
        pl.semaphore_wait(barrier, 12)
    with jax.named_scope("a1"):
        g_a.start1()
        tokens.start1()
        for copy in local[3:]:
            copy.wait()
        g_b.start1()
    with jax.named_scope("a2"):
        g_a.start2()
        g_c.start1()
    with jax.named_scope("b2"):
        g_b.start2()
    with jax.named_scope("a3"):
        g_a.start3()
    with jax.named_scope("a4"):
        g_a.start4()
        g_c.start2()
        g_b.start3()
        g_d.start1()
    with jax.named_scope("tokens2"):
        tokens.start2()
    with jax.named_scope("a5"):
        g_a.finish()
        tokens.own_chip()
    with jax.named_scope("own_a"):
        raw_product(0, w_a, 0)
    with jax.named_scope("b4"):
        g_b.start4()
        g_d.start2()
        g_c.start3()
        g_e.start1()
    with jax.named_scope("tokens3"):
        tokens.start3()
    with jax.named_scope("b5"):
        g_b.finish()
    with jax.named_scope("own_b"):
        raw_product(0, w_b, 1)
    with jax.named_scope("near_wait"):
        tokens.near_chips()
    with jax.named_scope("near_ab"):

        @pl.loop(0, 2)
        def _(i):
            raw_product(2 * i + 3, w_a, 0)
            raw_product(2 * i + 3, w_b, 1)

    with jax.named_scope("c4"):
        g_c.start4()
        g_e.start2()
        g_d.start3()
        o_a.start1()
    with jax.named_scope("tokens4"):
        tokens.start4()
    with jax.named_scope("far_wait"):
        tokens.far_chip()
    with jax.named_scope("far_ab"):
        raw_product(2, w_a, 0)
        raw_product(2, w_b, 1)
    with jax.named_scope("c5"):
        g_c.finish()
        g_e.start3()
    with jax.named_scope("all_c"):

        @pl.loop(0, 4)
        def _(i):
            raw_product(i, w_c, 2)

    with jax.named_scope("squares"):

        @pl.loop(0, 8)
        def _(b):
            rows = pl.ds(pl.multiple_of(b * 128, 128), 128)
            for part in range(2):
                p = raw[rows, part * LOCAL : (part + 1) * LOCAL]
                total = jnp.sum(p * p, axis=1, keepdims=True)
                row = jnp.sum(jnp.where(eye_mask(), total, 0.0), axis=0, keepdims=True)
                squares[me.head, pl.ds(part * 8 + b, 1), :] = row

        s_squares, r_squares = link.take(1, 1)
        for d in range(1, 8):
            own = squares.at[me.head]
            to = (me.step, (me.head + d) % 8, me.x_hi)
            link.copy(own, own, s_squares, r_squares, to).start()
    length = length_ref[0]

    def softmax(h, m):
        rows = pl.ds(pl.multiple_of(m * 256, 256), 256)
        valid = lax.broadcasted_iota(jnp.int32, (256, 512), 1) < length - 512
        q = qk[rows, h * HD : (h + 1) * HD]
        k = qk[:, LOCAL + h * HD : LOCAL + (h + 1) * HD]
        s = lax.dot_general(q, k, (((1,), (1,)), ((), ())), preferred_element_type=F32)
        s = s * (math.log2(math.e) / math.sqrt(HD))
        s = jnp.concatenate([s[:, 0:512], jnp.where(valid, s[:, 512:1024], -jnp.inf)], axis=1)
        probs[h, rows, :] = jnp.exp2(s - jnp.max(s, axis=-1, keepdims=True)).astype(BF16)

    def attend(h, m):
        rows = pl.ds(pl.multiple_of(m * 256, 256), 256)
        o = jnp.dot(probs[h, rows, :], value[h], preferred_element_type=F32)
        attended[rows, h * HD : (h + 1) * HD] = (o[:, 0:HD] / o[:, HD : 2 * HD]).astype(BF16)

    def value_product(w, heads, m):
        rows = pl.ds(pl.multiple_of(m * 256, 256), 256)
        v = product(rows, w).astype(BF16)
        for n, h in enumerate(heads):
            value[h, rows, 0:HD] = v[:, n * HD : (n + 1) * HD]

    with jax.named_scope("d4"):
        g_d.start4()
        o_a.start2()
        o_b.start1()
        g_e.start4()
    with jax.named_scope("squares_wait"):
        link.got(r_squares, squares.at[0:7])
        link.sent(s_squares, squares.at[0:7])

    with jax.named_scope("qk_norm"):

        @pl.loop(0, 8)
        def _(b):
            rows = pl.ds(pl.multiple_of(b * 128, 128), 128)
            for part, gain in enumerate((q_gain_ref, k_gain_ref)):
                total = squares[0, pl.ds(part * 8 + b, 1), :]
                for d in range(1, 8):
                    total = total + squares[d, pl.ds(part * 8 + b, 1), :]
                factor = lax.rsqrt(total / 3072.0 + 1e-06)
                column = jnp.sum(jnp.where(eye_mask(), factor, 0.0), axis=1, keepdims=True)
                cols = slice(part * LOCAL, (part + 1) * LOCAL)
                qk[rows, cols] = (raw[rows, cols] * column * gain[...].reshape(1, LOCAL)).astype(BF16)

    with jax.named_scope("softmax0"):

        @pl.loop(0, 4)
        def _(m):
            softmax(0, m)

    with jax.named_scope("o_a3"):
        o_a.start3()
        o_b.start2()
        o_c.start1()
    with jax.named_scope("d5"):
        g_d.finish()
    with jax.named_scope("softmax1_value_d"):

        @pl.loop(0, 4)
        def _(m):
            softmax(1, m)
            value_product(w_d, (0, 1), m)

    with jax.named_scope("o_b3"):
        o_a.start4()
        o_b.start3()
    with jax.named_scope("e5"):
        g_e.finish()
        o_c.start2()
    with jax.named_scope("softmax2_value_e"):

        @pl.loop(0, 4)
        def _(m):
            softmax(2, m)
            value_product(w_e, (2,), m)

    with jax.named_scope("o_b4"):
        o_b.start4()
        o_c.start3()
    with jax.named_scope("attend"):

        @pl.loop(0, 4)
        def _(m):
            for h in range(3):
                attend(h, m)

    with jax.named_scope("o_a5"):
        o_a.finish()
        for g in (g_a, g_b, g_c, g_d, g_e, tokens):
            g.drain()

    kinds = [link.take(FLIGHT, NJ if kind == 4 else AHEAD) for kind in range(6)]
    sib, first, second, pair, chain, back = range(6)
    up, down = me.at(dz=1), me.at(dz=-1)
    above, below, far = (me.z + 1) % 4, (me.z - 1) % 4, (me.z + 2) % 4
    partner = (me.y * 2 + 1 - me.x_lo, me.head, me.x_hi)
    later = [me.at(dy=d) for d in (1, 2, 3)]
    on_low = me.x_lo == 0
    lower = lax.broadcasted_iota(jnp.int32, (TOK, 128), 1) < 64
    width = (jnp.full((1, 128), time_ref[0, 1] - time_ref[0, 0], jnp.int32)).astype(F32) / 1000.0

    def send_of(kind, j):
        return kinds[kind][0] + j % FLIGHT

    def recv_of(kind, j):
        return kinds[kind][1] + (j if kind == chain else j % AHEAD)

    def go(kind, j, src, dst, to):
        link.copy(src, dst, send_of(kind, j), recv_of(kind, j), to).start()

    def got(kind, j, size):
        link.got(recv_of(kind, j), size)

    def sent(kind, j, size):
        link.sent(send_of(kind, j), size)

    def natural(j, m):
        piece, tile = j // 4, (j % 4) * 2 + m
        odd = piece % 2
        low = 5 * tile + (piece + 5 * odd) // 2
        high = 5 * tile + 2 * (1 - odd) + (piece - odd) // 2
        return (
            pl.ds(pl.multiple_of(low * 128, 128), 128),
            pl.ds(pl.multiple_of(high * 128, 128), 128),
        )

    def kept(j, half):
        start = (j % 8) * 128 + half * 64
        return pl.ds(pl.multiple_of(start, 64), 64), pl.ds(pl.multiple_of((j // 8) * 256, 256), 256)

    def project(j):
        w = o_full[j // 4, j % 4].reshape(CW, LOCAL)
        for m in range(4):
            p = lax.dot_general(
                attended[m * 256 : (m + 1) * 256, :],
                w,
                (((1,), (1,)), ((), ())),
                preferred_element_type=F32,
            ).astype(BF16)
            partial[j % SLOTS, m, 0] = p[0:128]
            partial[j % SLOTS, m, 1] = p[128:256]
        go(sib, j, partial.at[j % SLOTS, :, 1 - me.core], summed.at[j], me.at(other_core=True))

    def add_sibling(j):
        got(sib, j, summed.at[j])
        for m in range(4):
            own = partial[j % SLOTS, m, me.core].astype(F32)
            summed[j, m] = (own + summed[j, m].astype(F32)).astype(BF16)
        sent(sib, j, summed.at[j])
        go(first, j, summed.at[j, far, 0:64], z_first.at[j, 0], up)
        go(first, j, summed.at[j, far, 64:128], z_first.at[j, 1], down)

    def add_far(j):
        got(first, j, z_first.at[j])
        summed[j, above, 0:64] = (
            summed[j, above, 0:64].astype(F32) + z_first[j, 0].astype(F32)
        ).astype(BF16)
        summed[j, below, 64:128] = (
            summed[j, below, 64:128].astype(F32) + z_first[j, 1].astype(F32)
        ).astype(BF16)
        go(second, j, summed.at[j, above], z_second.at[j, 0], up)
        go(second, j, summed.at[j, below], z_second.at[j, 1], down)
        sent(first, j, z_first.at[j])

    def drift(j):
        got(second, j, z_second.at[j])
        rows = pl.ds(pl.multiple_of((j % 8) * 128, 128), 128)
        for m in range(2):
            lanes = slice(m * 128, (m + 1) * 128)
            total = (
                summed[j, me.z, :, lanes].astype(F32)
                + z_second[j, 0, :, lanes].astype(F32)
                + z_second[j, 1, :, lanes].astype(F32)
            )
            projected = jnp.where((j // 4) % 2 == 1, pltpu.roll(total, 64, 1), total)
            low, high = natural(j, m)
            gate = jnp.where(lower[0:1], mod[2, :, low], mod[2, :, high])
            branch = gate * projected
            update_ref[:, low] = jnp.where(lower, branch, update_ref[:, low].astype(F32)).astype(BF16)
            update_ref[:, high] = jnp.where(lower, update_ref[:, high].astype(F32), branch).astype(BF16)
            current = jnp.where(lower, states[:, low], states[:, high])
            anchor = jnp.where(me.step == 0, current, 0.0)
            raw[rows, pl.ds(pl.multiple_of((j // 8) * 256 + m * 128, 128), 128)] = (
                width * (current + branch) + anchor
            )
        pair_out[j] = raw[kept(j, 1 - me.x_lo)].astype(BF16)
        go(pair, j, pair_out.at[j], pair_in.at[j], partner)
        sent(second, j, z_second.at[j])

    def add_pair(j):
        got(pair, j, pair_in.at[j])
        chain_out[j] = (raw[kept(j, me.x_lo)] + pair_in[j].astype(F32)).astype(BF16)
        for d in (1, 2, 3):

            @pl.when(me.y + d < 4)
            def _(d=d):
                go(chain, j, chain_out.at[j], chain_in.at[j, d - 1], later[d - 1])

        sent(pair, j, pair_in.at[j])

    def add_earlier(j):
        for d in (1, 2, 3):

            @pl.when(me.y == d)
            def _(d=d):
                got(chain, j, chain_in.at[j, 0:d])

        earlier = jnp.zeros((64, CW), F32)
        for d in (1, 2, 3):
            earlier = earlier + jnp.where(me.y >= d, chain_in[j, d - 1].astype(F32), 0.0)
        mine = kept(j, me.x_lo)
        own = raw[mine]
        back_out[j] = (earlier + jnp.where(on_low, own, 0.0)).astype(BF16)
        go(back, j, back_out.at[j], back_in.at[j], partner)
        raw[mine] = own + (earlier + jnp.where(on_low, 0.0, pair_in[j].astype(F32)))
        for d in (1, 2, 3):

            @pl.when(me.y + d == 3)
            def _(d=d):
                sent(chain, j, chain_in.at[j, 0:d])

    def add_back(j):
        got(back, j, back_in.at[j])
        other = kept(j, 1 - me.x_lo)
        raw[other] = raw[other] + back_in[j].astype(F32)
        rows = pl.ds(pl.multiple_of((j % 8) * 128, 128), 128)
        for m in range(2):
            low, high = natural(j, m)
            total = raw[rows, pl.ds(pl.multiple_of((j // 8) * 256 + m * 128, 128), 128)]
            next_ref[:, low] = jnp.where(lower, total, next_ref[:, low])
            next_ref[:, high] = jnp.where(lower, next_ref[:, high], total)
        sent(back, j, back_in.at[j])

    with jax.named_scope("reduce"):
        stages = (project, add_sibling, add_far, drift, add_pair, add_earlier, add_back)

        @pl.loop(0, NJ + LAGS[-1])
        def _(i):
            @pl.when(i == 4)
            def _():
                o_b.finish()

            @pl.when(i == 6)
            def _():
                o_c.start4()

            @pl.when(i == 8)
            def _():
                o_c.finish()

            for lag, stage in zip(LAGS, stages):
                j = i - lag

                @pl.when((j >= 0) & (j < NJ))
                def _(stage=stage, j=j):
                    stage(j)

    with jax.named_scope("drain"):
        for g in (o_a, o_b, o_c):
            g.drain()


def body(states, timesteps, lengths, modulation, w_query, w_key, w_value, w_out, q_gain, k_gain):
    n_send = 8 * 4 + 6 + 1 + 6 * FLIGHT
    n_recv = 8 * 6 + 6 + 1 + 5 * AHEAD + NJ
    vmem = pl.BlockSpec(memory_space=pltpu.VMEM)
    smem = pl.BlockSpec(memory_space=pltpu.SMEM)
    anywhere = pl.BlockSpec(memory_space=pl.ANY)
    nxt, update = pl.pallas_call(
        kernel,
        out_shape=(
            pltpu.VMEM((TOK, 5120), F32),
            pltpu.VMEM((TOK, 5120), BF16),
        ),
        in_specs=[smem, smem, vmem, vmem] + [anywhere] * 6,
        out_specs=(vmem, vmem),
        scratch_shapes=[
            pltpu.VMEM((TOK, 5120), F32),
            pltpu.VMEM((3, 1, 5120), F32),
            pltpu.VMEM((1024, 5120), BF16),
            pltpu.VMEM((4, 4, 2, 160, 256), BF16),
            pltpu.VMEM((4, 4, 2, 160, 256), BF16),
            pltpu.VMEM((4, 4, 2, 160, 256), BF16),
            pltpu.VMEM((4, 4, 2, 160, 256), BF16),
            pltpu.VMEM((4, 4, 2, 160, 128), BF16),
            pltpu.VMEM((PIECES, 4, 4, 2, 32, LOCAL), BF16),
            pltpu.VMEM((1024, 2 * LOCAL), F32),
            pltpu.VMEM((1024, 2 * LOCAL), BF16),
            pltpu.VMEM((3, 1024, 2 * HD), BF16),
            pltpu.VMEM((3, 1024, 1024), BF16),
            pltpu.VMEM((1024, LOCAL), BF16),
            pltpu.VMEM((8, 16, 128), F32),
            pltpu.VMEM((SLOTS, 4, 2, TOK, CW), BF16),
            pltpu.VMEM((NJ, 4, TOK, CW), BF16),
            pltpu.VMEM((NJ, 2, 64, CW), BF16),
            pltpu.VMEM((NJ, 2, TOK, CW), BF16),
            pltpu.VMEM((NJ, 64, CW), BF16),
            pltpu.VMEM((NJ, 64, CW), BF16),
            pltpu.VMEM((NJ, 64, CW), BF16),
            pltpu.VMEM((NJ, 3, 64, CW), BF16),
            pltpu.VMEM((NJ, 64, CW), BF16),
            pltpu.VMEM((NJ, 64, CW), BF16),
            pltpu.SemaphoreType.DMA((n_send,)),
            pltpu.SemaphoreType.DMA((n_recv,)),
            pltpu.SemaphoreType.DMA((9,)),
        ],
        compiler_params=pltpu.CompilerParams(
            collective_id=0,
            has_side_effects=True,
            vmem_limit_bytes=57 * 1024 * 1024,
        ),
    )(
        lengths,
        timesteps,
        q_gain,
        k_gain,
        states,
        modulation.transpose(1, 0, 2),
        w_query.reshape(2, 160, LOCAL),
        w_key.reshape(2, 160, LOCAL),
        w_value.reshape(2, 160, LOCAL),
        w_out.T.reshape(PIECES, 2, 32, LOCAL),
    )
    return (nxt[None, None], update[None, None])


def solution(mesh):
    in_specs = (
        P("step", "fsdp", "head", None),
        P("step", None),
        P("fsdp"),
        P("step", None, None),
        P(("step", "fsdp"), "head"),
        P(("step", "fsdp"), "head"),
        P(("step", "fsdp"), "head"),
        P("head", ("step", "fsdp")),
        P("head"),
        P("head"),
    )
    out_specs = (P("step", "fsdp", "head", None), P("step", "fsdp", "head", None))
    return jax.shard_map(body, mesh=mesh, in_specs=in_specs, out_specs=out_specs, check_vma=False)
```

```python
import math

import jax
import jax.numpy as jnp
from jax import lax
from jax.experimental import pallas as pl
from jax.experimental.pallas import tpu as pltpu
from jax.sharding import PartitionSpec as P

HD = 128
BF16 = jnp.bfloat16
F32 = jnp.float32
MESH = pl.DeviceIdType.MESH
TOK = 128
LOCAL = 384
PIECES = 5
NJ = 20
CW = 256
LAGS = (0, 2, 5, 8, 10, 12, 14)
SLOTS = 3
FLIGHT = 4
AHEAD = 8


class Link:
    def __init__(self, send, recv, some_device):
        self.send, self.recv, self.to = send, recv, some_device
        self.sends, self.recvs = 0, 0

    def take(self, sends, recvs):
        first = self.sends, self.recvs
        self.sends, self.recvs = self.sends + sends, self.recvs + recvs
        return first

    def copy(self, src, dst, send, recv, to):
        return pltpu.make_async_remote_copy(
            src_ref=src,
            dst_ref=dst,
            send_sem=self.send.at[send],
            recv_sem=self.recv.at[recv],
            device_id=to,
            device_id_type=MESH,
        )

    def sent(self, send, size):
        self.copy(size, size, send, 0, self.to).wait_send()

    def got(self, recv, size):
        self.copy(size, size, 0, recv, self.to).wait_recv()


class Place:
    def __init__(self):
        step, head, fsdp = (lax.axis_index(a) for a in ("step", "head", "fsdp"))
        self.step, self.head = step, head
        self.y, self.x_lo, self.x_hi = step // 2, step % 2, fsdp
        self.x = self.x_hi * 2 + self.x_lo
        self.z, self.core = head // 2, head % 2

    def at(self, dx=0, dy=0, dz=0, other_core=False):
        x, y, z = (self.x + dx) % 4, (self.y + dy) % 4, (self.z + dz) % 4
        core = 1 - self.core if other_core else self.core
        return (y * 2 + x % 2, z * 2 + core, x // 2)

    def column(self, dx):
        x = (self.x + dx) % 4
        return (x % 2) * 2 + x // 2

    def row(self, dy):
        return (self.y + dy) % 4


class PlaneGather:
    def __init__(self, link, place, view, half):
        me = place
        whole, low, high = slice(0, half), slice(0, half // 2), slice(half // 2, half)
        every = slice(0, 4)
        y, c = me.y, me.column(0)
        left, right, far_x = me.column(-1), me.column(1), me.column(2)
        below, above, far_y = me.row(-1), me.row(1), me.row(2)
        east, west, north, south = me.at(dx=1), me.at(dx=-1), me.at(dy=1), me.at(dy=-1)
        self.link, self.view = link, view
        self.s, self.r = link.take(4, 4)
        self.sends = (
            ((y, c, 0, whole), east),
            ((y, c, 0, whole), west),
            ((y, c, 1, whole), north),
            ((y, c, 1, whole), south),
            ((y, left, 0, low), east),
            ((y, right, 0, high), west),
            ((below, c, 1, low), north),
            ((above, c, 1, high), south),
            ((y, every, 0, whole), north),
            ((y, every, 0, whole), south),
            ((every, c, 1, whole), east),
            ((every, c, 1, whole), west),
            ((below, every, 0, low), north),
            ((above, every, 0, high), south),
            ((every, left, 1, low), east),
            ((every, right, 1, high), west),
        )
        two = slice(0, 2)
        self.pair = view(y, two, 0, whole)
        self.rows = view(two, every, 0, whole)
        self.half = view(every, every, 0, whole)
        self.row = view(y, every, 0, whole)

    def start(self, first, last):
        for slot in range(first, last):
            args, to = self.sends[slot]
            part = self.view(*args)
            self.link.copy(part, part, self.s + slot // 4, self.r + slot // 4, to).start()

    def got(self, n, size):
        self.link.got(self.r + n, size)

    def start1(self):
        self.start(0, 4)

    def start2(self):
        self.got(0, self.row)
        self.start(4, 8)

    def start3(self):
        self.got(1, self.pair)
        self.start(8, 12)

    def start4(self):
        self.got(2, self.half)
        self.start(12, 16)

    def finish(self):
        self.got(3, self.rows)

    def drain(self):
        for phase, size in enumerate((self.row, self.pair, self.half, self.rows)):
            self.link.sent(self.s + phase, size)


class TokenGather:
    def __init__(self, link, place, acts):
        self.link, self.me, self.acts = link, place, acts
        self.s, self.r = link.take(6, 6)

    def rows(self, dz, start=0, size=TOK):
        me = self.me
        z = (me.z + dz) % 4
        return self.acts.at[pl.ds(pl.multiple_of((z * 2 + me.core) * TOK + start, 64), size), :]

    def low(self, dz):
        return self.rows(dz, 0, 64)

    def high(self, dz):
        return self.rows(dz, 64, 64)

    def go(self, n, part, to):
        self.link.copy(part, part, self.s + n, self.r + n, to).start()

    def got(self, n, rows=TOK):
        self.link.got(self.r + n, self.acts.at[0:rows])

    def start1(self):
        up, down = self.me.at(dz=1), self.me.at(dz=-1)
        self.go(0, self.low(0), up)
        self.go(0, self.high(0), down)
        self.go(1, self.high(0), up)
        self.go(1, self.low(0), down)
        self.go(2, self.rows(0), self.me.at(other_core=True))

    def start2(self):
        self.got(0)
        self.go(3, self.low(-1), self.me.at(dz=1))
        self.go(3, self.high(1), self.me.at(dz=-1))

    def start3(self):
        other = self.me.at(other_core=True)
        self.got(1)
        self.go(4, self.rows(-1), other)
        self.go(4, self.rows(1), other)

    def start4(self):
        self.got(3)
        self.go(5, self.rows(2), self.me.at(other_core=True))

    def own_chip(self):
        self.got(2)

    def near_chips(self):
        self.got(4, 2 * TOK)

    def far_chip(self):
        self.got(5)

    def drain(self):
        for n in range(6):
            self.link.sent(self.s + n, self.acts.at[0 : 2 * TOK if n == 4 else TOK])


def eye_mask():
    return lax.broadcasted_iota(jnp.int32, (128, 128), 0) == lax.broadcasted_iota(
        jnp.int32, (128, 128), 1
    )


def kernel(
    length_ref,
    time_ref,
    q_gain_ref,
    k_gain_ref,
    states_hbm,
    mod_hbm,
    wq_hbm,
    wk_hbm,
    wv_hbm,
    wo_hbm,
    next_ref,
    update_ref,
    states,
    mod,
    acts,
    w_a,
    w_b,
    w_c,
    w_d,
    w_e,
    o_full,
    raw,
    qk,
    value,
    probs,
    attended,
    squares,
    partial,
    summed,
    z_first,
    z_second,
    pair_out,
    pair_in,
    chain_out,
    chain_in,
    back_out,
    back_in,
    send_sem,
    recv_sem,
    local_sem,
):
    me = Place()
    link = Link(send_sem, recv_sem, me.at(dx=1))

    barrier = pltpu.get_barrier_semaphore()
    for d in range(1, 8):
        pl.semaphore_signal(
            barrier,
            inc=1,
            device_id=(me.step, (me.head + d) % 8, me.x_hi),
            device_id_type=MESH,
        )
    for to in [me.at(dx=1), me.at(dx=-1)] + [me.at(dy=d) for d in (1, 2, 3)]:
        pl.semaphore_signal(barrier, inc=1, device_id=to, device_id_type=MESH)

    y, c = me.y, me.column(0)
    local = []
    for src, dst in (
        (states_hbm.at[0, 0], states),
        (mod_hbm, mod),
        (wq_hbm.at[:, :, 0:256], w_a.at[y, c]),
        (wq_hbm.at[:, :, 256:384], w_b.at[y, c, :, :, 0:128]),
        (wk_hbm.at[:, :, 0:128], w_b.at[y, c, :, :, 128:256]),
        (wk_hbm.at[:, :, 128:384], w_c.at[y, c]),
        (wv_hbm.at[:, :, 0:256], w_d.at[y, c]),
        (wv_hbm.at[:, :, 256:384], w_e.at[y, c]),
        (wo_hbm, o_full.at[:, y, c]),
    ):
        copy = pltpu.make_async_copy(src, dst, local_sem.at[len(local)])
        copy.start()
        local.append(copy)

    def weight(full):
        return PlaneGather(link, me, lambda y, c, h, r: full.at[y, c, h, r], 160)

    def out_weight(first, last):
        return PlaneGather(link, me, lambda y, c, h, r: o_full.at[first:last, y, c, h, r], 32)

    g_a, g_b, g_c, g_d, g_e = (weight(w) for w in (w_a, w_b, w_c, w_d, w_e))
    o_a, o_b, o_c = out_weight(0, 1), out_weight(1, 2), out_weight(2, 5)
    tokens = TokenGather(link, me, acts)

    def product(rows, w):
        return jnp.dot(acts[rows, :], w[...].reshape(5120, w.shape[-1]), preferred_element_type=F32)

    def raw_product(dz, w, column):
        rows = pl.ds(pl.multiple_of(((me.z + dz) % 4) * 256, 256), 256)
        raw[rows, column * 256 : column * 256 + 256] = product(rows, w)

    with jax.named_scope("norm"):
        local[0].wait()
        local[1].wait()
        shift, scale = mod[0], 1.0 + mod[1]

        @pl.loop(0, 4)
        def _(r):
            x = states[pl.ds(pl.multiple_of(r * 32, 32), 32), :]
            centred = x - jnp.mean(x, axis=-1, keepdims=True)
            spread = jnp.mean(centred * centred, axis=-1, keepdims=True)
            out = centred * lax.rsqrt(spread + 1e-06) * scale + shift
            acts[pl.ds(pl.multiple_of(me.head * TOK + r * 32, 32), 32), :] = out.astype(BF16)

        for h in range(3):
            value[h, :, HD : 2 * HD] = jnp.ones((1024, HD), BF16)

    with jax.named_scope("barrier"):
        local[2].wait()
        pl.semaphore_wait(barrier, 12)
    with jax.named_scope("a1"):
        g_a.start1()
        tokens.start1()
        for copy in local[3:]:
            copy.wait()
        g_b.start1()
    with jax.named_scope("a2"):
        g_a.start2()
        g_c.start1()
    with jax.named_scope("b2"):
        g_b.start2()
    with jax.named_scope("a3"):
        g_a.start3()
    with jax.named_scope("a4"):
        g_a.start4()
        g_c.start2()
        g_b.start3()
        g_d.start1()
    with jax.named_scope("tokens2"):
        tokens.start2()
    with jax.named_scope("a5"):
        g_a.finish()
        tokens.own_chip()
    with jax.named_scope("own_a"):
        raw_product(0, w_a, 0)
    with jax.named_scope("b4"):
        g_b.start4()
        g_d.start2()
        g_c.start3()
        g_e.start1()
    with jax.named_scope("tokens3"):
        tokens.start3()
    with jax.named_scope("b5"):
        g_b.finish()
    with jax.named_scope("own_b"):
        raw_product(0, w_b, 1)
    with jax.named_scope("near_wait"):
        tokens.near_chips()
    with jax.named_scope("near_ab"):

        @pl.loop(0, 2)
        def _(i):
            raw_product(2 * i + 3, w_a, 0)
            raw_product(2 * i + 3, w_b, 1)

    with jax.named_scope("c4"):
        g_c.start4()
        g_e.start2()
        g_d.start3()
        o_a.start1()
    with jax.named_scope("tokens4"):
        tokens.start4()
    with jax.named_scope("far_wait"):
        tokens.far_chip()
    with jax.named_scope("far_ab"):
        raw_product(2, w_a, 0)
        raw_product(2, w_b, 1)
    with jax.named_scope("c5"):
        g_c.finish()
        g_e.start3()
    with jax.named_scope("all_c"):

        @pl.loop(0, 4)
        def _(i):
            raw_product(i, w_c, 2)

    with jax.named_scope("squares"):

        @pl.loop(0, 8)
        def _(b):
            rows = pl.ds(pl.multiple_of(b * 128, 128), 128)
            for part in range(2):
                p = raw[rows, part * LOCAL : (part + 1) * LOCAL]
                total = jnp.sum(p * p, axis=1, keepdims=True)
                row = jnp.sum(jnp.where(eye_mask(), total, 0.0), axis=0, keepdims=True)
                squares[me.head, pl.ds(part * 8 + b, 1), :] = row

        s_squares, r_squares = link.take(1, 1)
        for d in range(1, 8):
            own = squares.at[me.head]
            to = (me.step, (me.head + d) % 8, me.x_hi)
            link.copy(own, own, s_squares, r_squares, to).start()
    length = length_ref[0]

    def softmax(h, m):
        rows = pl.ds(pl.multiple_of(m * 256, 256), 256)
        valid = lax.broadcasted_iota(jnp.int32, (256, 512), 1) < length - 512
        q = qk[rows, h * HD : (h + 1) * HD]
        k = qk[:, LOCAL + h * HD : LOCAL + (h + 1) * HD]
        s = lax.dot_general(q, k, (((1,), (1,)), ((), ())), preferred_element_type=F32)
        s = s * (math.log2(math.e) / math.sqrt(HD))
        s = jnp.concatenate([s[:, 0:512], jnp.where(valid, s[:, 512:1024], -jnp.inf)], axis=1)
        probs[h, rows, :] = jnp.exp2(s - jnp.max(s, axis=-1, keepdims=True)).astype(BF16)

    def attend(h, m):
        rows = pl.ds(pl.multiple_of(m * 256, 256), 256)
        o = jnp.dot(probs[h, rows, :], value[h], preferred_element_type=F32)
        attended[rows, h * HD : (h + 1) * HD] = (o[:, 0:HD] / o[:, HD : 2 * HD]).astype(BF16)

    def value_product(w, heads, m):
        rows = pl.ds(pl.multiple_of(m * 256, 256), 256)
        v = product(rows, w).astype(BF16)
        for n, h in enumerate(heads):
            value[h, rows, 0:HD] = v[:, n * HD : (n + 1) * HD]

    with jax.named_scope("d4"):
        g_d.start4()
        o_a.start2()
        o_b.start1()
        g_e.start4()
    with jax.named_scope("squares_wait"):
        link.got(r_squares, squares.at[0:7])
        link.sent(s_squares, squares.at[0:7])

    with jax.named_scope("qk_norm"):

        @pl.loop(0, 8)
        def _(b):
            rows = pl.ds(pl.multiple_of(b * 128, 128), 128)
            for part, gain in enumerate((q_gain_ref, k_gain_ref)):
                total = squares[0, pl.ds(part * 8 + b, 1), :]
                for d in range(1, 8):
                    total = total + squares[d, pl.ds(part * 8 + b, 1), :]
                factor = lax.rsqrt(total / 3072.0 + 1e-06)
                column = jnp.sum(jnp.where(eye_mask(), factor, 0.0), axis=1, keepdims=True)
                cols = slice(part * LOCAL, (part + 1) * LOCAL)
                qk[rows, cols] = (raw[rows, cols] * column * gain[...].reshape(1, LOCAL)).astype(BF16)

    with jax.named_scope("softmax0"):

        @pl.loop(0, 4)
        def _(m):
            softmax(0, m)

    with jax.named_scope("o_a3"):
        o_a.start3()
        o_b.start2()
        o_c.start1()
    with jax.named_scope("d5"):
        g_d.finish()
    with jax.named_scope("softmax1_value_d"):

        @pl.loop(0, 4)
        def _(m):
            softmax(1, m)
            value_product(w_d, (0, 1), m)

    with jax.named_scope("o_b3"):
        o_a.start4()
        o_b.start3()
    with jax.named_scope("e5"):
        g_e.finish()
        o_c.start2()
    with jax.named_scope("softmax2_value_e"):

        @pl.loop(0, 4)
        def _(m):
            softmax(2, m)
            value_product(w_e, (2,), m)

    with jax.named_scope("o_b4"):
        o_b.start4()
        o_c.start3()
    with jax.named_scope("attend"):

        @pl.loop(0, 4)
        def _(m):
            for h in range(3):
                attend(h, m)

    with jax.named_scope("o_a5"):
        o_a.finish()
        for g in (g_a, g_b, g_c, g_d, g_e, tokens):
            g.drain()

    kinds = [link.take(FLIGHT, NJ if kind == 4 else AHEAD) for kind in range(6)]
    sib, first, second, pair, chain, back = range(6)
    up, down = me.at(dz=1), me.at(dz=-1)
    above, below, far = (me.z + 1) % 4, (me.z - 1) % 4, (me.z + 2) % 4
    partner = (me.y * 2 + 1 - me.x_lo, me.head, me.x_hi)
    later = [me.at(dy=d) for d in (1, 2, 3)]
    on_low = me.x_lo == 0
    lower = lax.broadcasted_iota(jnp.int32, (TOK, 128), 1) < 64
    width = (jnp.full((1, 128), time_ref[0, 1] - time_ref[0, 0], jnp.int32)).astype(F32) / 1000.0

    def send_of(kind, j):
        return kinds[kind][0] + j % FLIGHT

    def recv_of(kind, j):
        return kinds[kind][1] + (j if kind == chain else j % AHEAD)

    def go(kind, j, src, dst, to):
        link.copy(src, dst, send_of(kind, j), recv_of(kind, j), to).start()

    def got(kind, j, size):
        link.got(recv_of(kind, j), size)

    def sent(kind, j, size):
        link.sent(send_of(kind, j), size)

    def natural(j, m):
        piece, tile = j // 4, (j % 4) * 2 + m
        odd = piece % 2
        low = 5 * tile + (piece + 5 * odd) // 2
        high = 5 * tile + 2 * (1 - odd) + (piece - odd) // 2
        return (
            pl.ds(pl.multiple_of(low * 128, 128), 128),
            pl.ds(pl.multiple_of(high * 128, 128), 128),
        )

    def kept(j, half):
        start = (j % 8) * 128 + half * 64
        return pl.ds(pl.multiple_of(start, 64), 64), pl.ds(pl.multiple_of((j // 8) * 256, 256), 256)

    def project(j):
        w = o_full[j // 4, j % 4].reshape(CW, LOCAL)
        for m in range(4):
            p = lax.dot_general(
                attended[m * 256 : (m + 1) * 256, :],
                w,
                (((1,), (1,)), ((), ())),
                preferred_element_type=F32,
            ).astype(BF16)
            partial[j % SLOTS, m, 0] = p[0:128]
            partial[j % SLOTS, m, 1] = p[128:256]
        go(sib, j, partial.at[j % SLOTS, :, 1 - me.core], summed.at[j], me.at(other_core=True))

    def add_sibling(j):
        got(sib, j, summed.at[j])
        for m in range(4):
            own = partial[j % SLOTS, m, me.core].astype(F32)
            summed[j, m] = (own + summed[j, m].astype(F32)).astype(BF16)
        sent(sib, j, summed.at[j])
        go(first, j, summed.at[j, far, 0:64], z_first.at[j, 0], up)
        go(first, j, summed.at[j, far, 64:128], z_first.at[j, 1], down)

    def add_far(j):
        got(first, j, z_first.at[j])
        summed[j, above, 0:64] = (
            summed[j, above, 0:64].astype(F32) + z_first[j, 0].astype(F32)
        ).astype(BF16)
        summed[j, below, 64:128] = (
            summed[j, below, 64:128].astype(F32) + z_first[j, 1].astype(F32)
        ).astype(BF16)
        go(second, j, summed.at[j, above], z_second.at[j, 0], up)
        go(second, j, summed.at[j, below], z_second.at[j, 1], down)
        sent(first, j, z_first.at[j])

    def drift(j):
        got(second, j, z_second.at[j])
        rows = pl.ds(pl.multiple_of((j % 8) * 128, 128), 128)
        for m in range(2):
            lanes = slice(m * 128, (m + 1) * 128)
            total = (
                summed[j, me.z, :, lanes].astype(F32)
                + z_second[j, 0, :, lanes].astype(F32)
                + z_second[j, 1, :, lanes].astype(F32)
            )
            projected = jnp.where((j // 4) % 2 == 1, pltpu.roll(total, 64, 1), total)
            low, high = natural(j, m)
            gate = jnp.where(lower[0:1], mod[2, :, low], mod[2, :, high])
            branch = gate * projected
            update_ref[:, low] = jnp.where(lower, branch, update_ref[:, low].astype(F32)).astype(BF16)
            update_ref[:, high] = jnp.where(lower, update_ref[:, high].astype(F32), branch).astype(BF16)
            current = jnp.where(lower, states[:, low], states[:, high])
            anchor = jnp.where(me.step == 0, current, 0.0)
            raw[rows, pl.ds(pl.multiple_of((j // 8) * 256 + m * 128, 128), 128)] = (
                width * (current + branch) + anchor
            )
        pair_out[j] = raw[kept(j, 1 - me.x_lo)].astype(BF16)
        go(pair, j, pair_out.at[j], pair_in.at[j], partner)
        sent(second, j, z_second.at[j])

    def add_pair(j):
        got(pair, j, pair_in.at[j])
        chain_out[j] = (raw[kept(j, me.x_lo)] + pair_in[j].astype(F32)).astype(BF16)
        for d in (1, 2, 3):

            @pl.when(me.y + d < 4)
            def _(d=d):
                go(chain, j, chain_out.at[j], chain_in.at[j, d - 1], later[d - 1])

        sent(pair, j, pair_in.at[j])

    def add_earlier(j):
        for d in (1, 2, 3):

            @pl.when(me.y == d)
            def _(d=d):
                got(chain, j, chain_in.at[j, 0:d])

        earlier = jnp.zeros((64, CW), F32)
        for d in (1, 2, 3):
            earlier = earlier + jnp.where(me.y >= d, chain_in[j, d - 1].astype(F32), 0.0)
        mine = kept(j, me.x_lo)
        own = raw[mine]
        back_out[j] = (earlier + jnp.where(on_low, own, 0.0)).astype(BF16)
        go(back, j, back_out.at[j], back_in.at[j], partner)
        raw[mine] = own + (earlier + jnp.where(on_low, 0.0, pair_in[j].astype(F32)))
        for d in (1, 2, 3):

            @pl.when(me.y + d == 3)
            def _(d=d):
                sent(chain, j, chain_in.at[j, 0:d])

    def add_back(j):
        got(back, j, back_in.at[j])
        other = kept(j, 1 - me.x_lo)
        raw[other] = raw[other] + back_in[j].astype(F32)
        rows = pl.ds(pl.multiple_of((j % 8) * 128, 128), 128)
        for m in range(2):
            low, high = natural(j, m)
            total = raw[rows, pl.ds(pl.multiple_of((j // 8) * 256 + m * 128, 128), 128)]
            next_ref[:, low] = jnp.where(lower, total, next_ref[:, low])
            next_ref[:, high] = jnp.where(lower, next_ref[:, high], total)
        sent(back, j, back_in.at[j])

    with jax.named_scope("reduce"):
        stages = (project, add_sibling, add_far, drift, add_pair, add_earlier, add_back)

        @pl.loop(0, NJ + LAGS[-1])
        def _(i):
            @pl.when(i == 4)
            def _():
                o_b.finish()

            @pl.when(i == 6)
            def _():
                o_c.start4()

            @pl.when(i == 8)
            def _():
                o_c.finish()

            for lag, stage in zip(LAGS, stages):
                j = i - lag

                @pl.when((j >= 0) & (j < NJ))
                def _(stage=stage, j=j):
                    stage(j)

    with jax.named_scope("drain"):
        for g in (o_a, o_b, o_c):
            g.drain()


def body(states, timesteps, lengths, modulation, w_query, w_key, w_value, w_out, q_gain, k_gain):
    n_send = 8 * 4 + 6 + 1 + 6 * FLIGHT
    n_recv = 8 * 4 + 6 + 1 + 5 * AHEAD + NJ
    vmem = pl.BlockSpec(memory_space=pltpu.VMEM)
    smem = pl.BlockSpec(memory_space=pltpu.SMEM)
    anywhere = pl.BlockSpec(memory_space=pl.ANY)
    nxt, update = pl.pallas_call(
        kernel,
        out_shape=(
            pltpu.VMEM((TOK, 5120), F32),
            pltpu.VMEM((TOK, 5120), BF16),
        ),
        in_specs=[smem, smem, vmem, vmem] + [anywhere] * 6,
        out_specs=(vmem, vmem),
        scratch_shapes=[
            pltpu.VMEM((TOK, 5120), F32),
            pltpu.VMEM((3, 1, 5120), F32),
            pltpu.VMEM((1024, 5120), BF16),
            pltpu.VMEM((4, 4, 2, 160, 256), BF16),
            pltpu.VMEM((4, 4, 2, 160, 256), BF16),
            pltpu.VMEM((4, 4, 2, 160, 256), BF16),
            pltpu.VMEM((4, 4, 2, 160, 256), BF16),
            pltpu.VMEM((4, 4, 2, 160, 128), BF16),
            pltpu.VMEM((PIECES, 4, 4, 2, 32, LOCAL), BF16),
            pltpu.VMEM((1024, 2 * LOCAL), F32),
            pltpu.VMEM((1024, 2 * LOCAL), BF16),
            pltpu.VMEM((3, 1024, 2 * HD), BF16),
            pltpu.VMEM((3, 1024, 1024), BF16),
            pltpu.VMEM((1024, LOCAL), BF16),
            pltpu.VMEM((8, 16, 128), F32),
            pltpu.VMEM((SLOTS, 4, 2, TOK, CW), BF16),
            pltpu.VMEM((NJ, 4, TOK, CW), BF16),
            pltpu.VMEM((NJ, 2, 64, CW), BF16),
            pltpu.VMEM((NJ, 2, TOK, CW), BF16),
            pltpu.VMEM((NJ, 64, CW), BF16),
            pltpu.VMEM((NJ, 64, CW), BF16),
            pltpu.VMEM((NJ, 64, CW), BF16),
            pltpu.VMEM((NJ, 3, 64, CW), BF16),
            pltpu.VMEM((NJ, 64, CW), BF16),
            pltpu.VMEM((NJ, 64, CW), BF16),
            pltpu.SemaphoreType.DMA((n_send,)),
            pltpu.SemaphoreType.DMA((n_recv,)),
            pltpu.SemaphoreType.DMA((9,)),
        ],
        compiler_params=pltpu.CompilerParams(
            collective_id=0,
            has_side_effects=True,
            vmem_limit_bytes=57 * 1024 * 1024,
        ),
    )(
        lengths,
        timesteps,
        q_gain,
        k_gain,
        states,
        modulation.transpose(1, 0, 2),
        w_query.reshape(2, 160, LOCAL),
        w_key.reshape(2, 160, LOCAL),
        w_value.reshape(2, 160, LOCAL),
        w_out.T.reshape(PIECES, 2, 32, LOCAL),
    )
    return (nxt[None, None], update[None, None])


def solution(mesh):
    in_specs = (
        P("step", "fsdp", "head", None),
        P("step", None),
        P("fsdp"),
        P("step", None, None),
        P(("step", "fsdp"), "head"),
        P(("step", "fsdp"), "head"),
        P(("step", "fsdp"), "head"),
        P("head", ("step", "fsdp")),
        P("head"),
        P("head"),
    )
    out_specs = (P("step", "fsdp", "head", None), P("step", "fsdp", "head", None))
    return jax.shard_map(body, mesh=mesh, in_specs=in_specs, out_specs=out_specs, check_vma=False)
```
